32 devices in a mesh: ctx: 2 (over x), user: 16 (over z, y, core).
Axes of the slice: x: 2, y: 2, z: 4, core: 2. Of those that a mesh axis runs over, the one named last changes fastest.
Arguments:
- queries: bfloat16 [16, 512, 512], P('user', 'ctx'), may hold values from -6 to 6
- key_rows: bfloat16 [16, 512, 512], P('user', 'ctx'), may hold values from -6 to 6
- value_rows: bfloat16 [16, 512, 512], P('user', 'ctx'), may hold values from -6 to 6
- gate_rows: bfloat16 [16, 512, 512], P('user', 'ctx'), may hold values from -6 to 6
- item_emb: bfloat16 [16, 512, 1024], P('user', 'ctx'), may hold values from -0.1875 to 0.1875
- labels: int32 [16, 512], P('user', 'ctx'), may hold values 0 or 1
- propensity: float32 [16, 512], P('user', 'ctx'), may hold values from 0.05 to 1
- requests: int32 [16, 512], P('user', 'ctx'), may hold values from 0 to 63, never falling along the last dimension, each value on 1 to 16 neighbouring positions
- lengths: int32 [16], P('user'), may hold values from 1 to 512, as said below
- w_out: bfloat16 [512, 1024], P(None, 'ctx'), may hold values from -0.25 to 0.25
Outputs:
- grad_query: float32 [16, 512, 512], P('user', 'ctx')
- grad_key: float32 [16, 512, 512], P('user', 'ctx')
- grad_value: float32 [16, 512, 512], P('user', 'ctx')
- grad_gate: float32 [16, 512, 512], P('user', 'ctx')
- grad_w_out: float32 [512, 1024], P('ctx', 'user')
The draws below stay inside these ranges and needn't reach their ends.
Inputs may be any that keep to these rules, and one draw needn't show every extreme that they name: `lengths`: every history has at least one live event and some history has all 512 events live. `requests`: request ids never fall along a history; a request spans at most 16 events.
All inputs are finite; a program needn't handle non-finite values. No bound on the sum of `labels` on one device may be relied on, other than what follows from the above.
Results may differ from the reference program's by a relative error of at most 0.0056.
Values may be sent and summed in bfloat16 or wider, within the bound.
A program may use at most 64 MiB of HBM per device.

```python
import math
import jax
import jax.numpy as jnp
import numpy as np
from jax import lax

D = 1024
HEADS = 4
HEAD_DIM = 128
REQS = 64
ATTN = 512
SEQ = 512
USERS = 16


def draw_lengths(key, part):
    key = jax.random.fold_in(key, 7)
    first_key, second_key = jax.random.split(key)
    drawn = jax.random.randint(first_key, (USERS,), 1, SEQ + 1)
    full_at = jax.random.randint(second_key, (), 0, USERS)
    return jnp.where(jnp.arange(USERS) == full_at, SEQ, drawn).astype(jnp.int32)


def plant(values, key, least, high):
    index_at = [jax.random.randint(jax.random.fold_in(key, axis), (), 0, length) for axis, length in enumerate(values.shape)]
    longest = values.shape.index(max(values.shape))
    neighbour = index_at[:longest] + [(index_at[longest] + 1) % values.shape[longest]] + index_at[longest + 1:]
    return values.at[tuple(index_at)].set(least).at[tuple(neighbour)].set(high)


def level_of(rng, shape, shards, low, high):
    def one(dim, shards_of):
        heights = jax.random.uniform(jax.random.fold_in(jax.random.fold_in(rng, 6), dim), (shards_of,), jnp.float32, low / len(shards), high / len(shards))
        return jnp.repeat(jnp.exp(heights), shape[dim] // shards_of).reshape((-1,) + (1,) * (len(shape) - dim - 1))

    factor_of = one(*shards[0])
    for cut in shards[1:]:
        factor_of = factor_of * one(*cut)
    return factor_of


def length_profile(amount, total, limit, slope):
    portions = [(1 << 20) // math.isqrt(standing ** slope) + 1 for standing in range(2, amount + 1)]
    rest, counts = total - limit - (amount - 1), [1] * (amount - 1)
    while rest > 0:
        free = [i for i in range(amount - 1) if counts[i] < limit]
        mass, remaining = sum([portions[i] for i in free]), rest
        for i in free:
            more = min(limit - counts[i], max(1, remaining * portions[i] // mass), rest)
            counts[i] = counts[i] + more
            rest = rest - more
    return np.array([limit] + counts)


def ragged(rng, amount, total, reach, skew):
    if amount == 2:
        one = jax.random.randint(rng, (), max(1, total - reach), min(reach, total - 1) + 1)
        return jnp.stack([one, total - one])
    tallies = jnp.asarray(length_profile(amount, total, reach, skew), jnp.int32)
    pairs = (amount - 1) // 2
    source_of, sink = tallies[1:1 + 2 * pairs:2], tallies[2:2 + 2 * pairs:2]
    room = jnp.minimum(source_of - 1, reach - sink)
    shifted = jax.random.randint(jax.random.fold_in(rng, 1), (pairs,), 0, 1 << 20) % (room + 1)
    tallies = tallies.at[1:1 + 2 * pairs:2].set(source_of - shifted).at[2:2 + 2 * pairs:2].set(sink + shifted)
    return tallies[jax.random.permutation(jax.random.fold_in(rng, 2), amount)]


def scatter_about(stream_key, dims, width, most, shards=(), kind=jnp.bfloat16):
    values = jax.random.normal(stream_key, dims, jnp.float32) * width
    if len(shards) > 0:
        values = level_of(stream_key, dims, shards, -0.22, 0.18) * values
    return jnp.clip(values, min=-most, max=most).astype(kind)


def setup_inputs(seed: int = 0) -> dict:
    key_list = jax.random.split(jax.random.key(seed), 11)
    queries = scatter_about(key_list[0], (USERS, SEQ, ATTN), 1.0, 6.0, ((0, 16), (1, 2)))
    key_rows = scatter_about(key_list[1], (USERS, SEQ, ATTN), 1.0, 6.0, ((0, 16), (1, 2)))
    value_rows = scatter_about(key_list[2], (USERS, SEQ, ATTN), 1.0, 6.0, ((0, 16), (1, 2)))
    gate_rows = scatter_about(key_list[3], (USERS, SEQ, ATTN), 1.0, 6.0, ((0, 16), (1, 2)))
    item_emb = scatter_about(key_list[4], (USERS, SEQ, D), D ** -0.5, 0.1875, ((0, 16), (1, 2)))
    labels = plant((jax.random.randint(key_list[5], (USERS, SEQ), 0, 4) < 1).astype(jnp.int32), jax.random.fold_in(key_list[5], 1), 0, 1)
    propensity = jnp.clip(jnp.exp(math.log(1.0) - 2.9957323 * jax.random.uniform(key_list[6], (USERS, SEQ), jnp.float32) ** level_of(key_list[6], (USERS, SEQ), ((0, 16), (1, 2)), -0.2, 0.2)), 0.05, 1.0)
    requests = jax.vmap(lambda own: jnp.searchsorted(jnp.cumsum(ragged(own, REQS, SEQ, 2 * SEQ // REQS, 2)), jnp.arange(SEQ), side="right"))(jax.random.split(key_list[7], USERS)).reshape((USERS, SEQ)).astype(jnp.int32)
    lengths = draw_lengths(jax.random.fold_in(key_list[10], 71), 0)
    w_out = scatter_about(key_list[9], (ATTN, D), ATTN ** -0.5, 0.25, ((1, 2),))
    return {"queries": queries, "key_rows": key_rows, "value_rows": value_rows, "gate_rows": gate_rows, "item_emb": item_emb, "labels": labels, "propensity": propensity, "requests": requests, "lengths": lengths, "w_out": w_out}


norm_eps = 1e-06

def silu_slope(values):
    sigmoid_v = jax.nn.sigmoid(values)
    return sigmoid_v * (1.0 + values * (1.0 - sigmoid_v))

def round_keep(values):
    return lax.optimization_barrier(values.astype(jnp.bfloat16)).astype(jnp.float32)

def user_backward(queries, key_rows, value_rows, gate_rows, item_emb, labels, propensity, requests, length, w_out):
    seq_len = queries.shape[0]
    feat_width = queries.shape[1]
    score_factor = 1.0 / math.sqrt(HEAD_DIM)
    query_f = queries.astype(jnp.float32).reshape(seq_len, HEADS, HEAD_DIM)
    key_f = key_rows.astype(jnp.float32).reshape(seq_len, HEADS, HEAD_DIM)
    value_f = value_rows.astype(jnp.float32).reshape(seq_len, HEADS, HEAD_DIM)
    gate_f = gate_rows.astype(jnp.float32)
    positions = jnp.arange(seq_len, dtype=jnp.int32)
    is_live = positions < length
    allowed = (positions[None, :] <= positions[:, None]) & is_live[None, :]
    scores = jnp.einsum('qhd,khd->hqk', query_f, key_f) * score_factor
    weights = round_keep(jnp.where(allowed[None], jax.nn.silu(scores), 0.0) / SEQ)
    attended = jnp.einsum('hqk,khd->qhd', weights, value_f).reshape(seq_len, feat_width)
    row_mean = lax.optimization_barrier(jnp.mean(attended, axis=-1, keepdims=True))
    centered = attended - row_mean
    variance = lax.optimization_barrier(jnp.mean(centered * centered, axis=-1, keepdims=True))
    inv_std = lax.rsqrt(variance + norm_eps)
    normed = centered * inv_std
    mixed_out = (normed * gate_f).astype(jnp.bfloat16)
    projected = jnp.dot(mixed_out, w_out, preferred_element_type=jnp.float32)
    logits = lax.optimization_barrier(jnp.sum(projected * item_emb.astype(jnp.float32), axis=-1))
    onehot = (requests[:, None] == jnp.arange(REQS, dtype=jnp.int32)[None, :]).astype(jnp.float32)
    live_f = is_live.astype(jnp.float32)
    inv_prop = jnp.where(is_live, 1.0 / propensity, 0.0)
    inv_sum = lax.optimization_barrier(jnp.sum(onehot * inv_prop[:, None], axis=0))
    live_count = lax.optimization_barrier(jnp.sum(onehot * live_f[:, None], axis=0))
    ratio = jnp.where(live_count > 0, live_count / jnp.where(live_count > 0, inv_sum, 1.0), 0.0)
    event_weight = inv_prop * lax.optimization_barrier(jnp.sum(onehot * ratio[None, :], axis=-1))
    grad_logits = event_weight * (jax.nn.sigmoid(logits) - labels.astype(jnp.float32))
    grad_proj = (grad_logits[:, None] * item_emb.astype(jnp.float32)).astype(jnp.bfloat16)
    grad_w = jnp.dot(mixed_out.T, grad_proj, preferred_element_type=jnp.float32)
    grad_mixed = jnp.dot(grad_proj, w_out.T, preferred_element_type=jnp.float32)
    grad_gate = grad_mixed * normed
    grad_normed = grad_mixed * gate_f
    grad_attn = (grad_normed - lax.optimization_barrier(jnp.mean(grad_normed, axis=-1, keepdims=True)) - normed * lax.optimization_barrier(jnp.mean(grad_normed * normed, axis=-1, keepdims=True))) * inv_std
    grad_attn = round_keep(grad_attn).reshape(seq_len, HEADS, HEAD_DIM)
    grad_weights = jnp.einsum('qhd,khd->hqk', grad_attn, value_f)
    grad_scores = round_keep(jnp.where(allowed[None], grad_weights * silu_slope(scores), 0.0) / SEQ)
    grad_query = jnp.einsum('hqk,khd->qhd', grad_scores, key_f) * score_factor
    grad_key = jnp.einsum('hqk,qhd->khd', grad_scores, query_f) * score_factor
    grad_value = jnp.einsum('hqk,qhd->khd', weights, grad_attn)
    return (grad_query.reshape(seq_len, feat_width), grad_key.reshape(seq_len, feat_width), grad_value.reshape(seq_len, feat_width), grad_gate, grad_w)

def reference(queries, key_rows, value_rows, gate_rows, item_emb, labels, propensity, requests, lengths, w_out):

    def per_user(grad_total, inputs):
        result = user_backward(*inputs, w_out)
        return (grad_total + result[4], result[:4])
    init_grad = jnp.zeros((HEADS * HEAD_DIM, D), jnp.float32)
    grad_w, outputs = lax.scan(per_user, init_grad, (queries, key_rows, value_rows, gate_rows, item_emb, labels, propensity, requests, lengths))
    return (outputs[0], outputs[1], outputs[2], outputs[3], grad_w)
```

```python
import functools
import math

import jax
import jax.numpy as jnp
from jax import lax
from jax.experimental import pallas as pl
from jax.experimental.pallas import tpu as pltpu
from jax.sharding import PartitionSpec as P

HEADS = 4
HEAD_DIM = 128
REQS = 64


norm_eps = 1e-06


def silu_slope(values):
    sigmoid_v = jax.nn.sigmoid(values)
    return sigmoid_v * (1.0 + values * (1.0 - sigmoid_v))


def split_heads(block):
    return block.reshape(block.shape[0], HEADS, HEAD_DIM)


def local(
    queries, key_rows, value_rows, gate_rows, item_emb, labels, propensity, requests, lengths, w_out
):
    row_count = queries.shape[1]
    feat_width = queries.shape[2]
    groups = lax.axis_size("ctx")
    seq_len = row_count * groups
    offset = lax.axis_index("ctx") * row_count
    score_factor = 1.0 / math.sqrt(HEAD_DIM)
    own_query = queries[0]
    own_key = key_rows[0]
    own_value = value_rows[0]
    query_h = split_heads(own_query)
    key_h = split_heads(own_key)
    value_h = split_heads(own_value)
    gate_f = gate_rows[0].astype(jnp.float32)
    hist_len = lengths[0]
    own_pos = offset + jnp.arange(row_count, dtype=jnp.int32)
    is_live = own_pos < hist_len
    key_piece = lax.all_gather(own_key, "ctx", axis=0, tiled=True)
    value_piece = lax.all_gather(own_value, "ctx", axis=0, tiled=True)
    piece_len = key_piece.shape[0]
    key_pos = jnp.arange(piece_len, dtype=jnp.int32)
    scores = (
        jnp.einsum(
            "qhd,khd->hqk", query_h, split_heads(key_piece), preferred_element_type=jnp.float32
        )
        * score_factor
    )
    allowed = (key_pos[None, :] <= own_pos[:, None]) & (key_pos[None, :] < hist_len)
    weights = (jnp.where(allowed[None], jax.nn.silu(scores), 0.0) / seq_len).astype(jnp.bfloat16)
    added = jnp.einsum(
        "hqk,khd->qhd", weights, split_heads(value_piece), preferred_element_type=jnp.float32
    )
    attended = added.reshape(row_count, feat_width)
    row_mean = jnp.mean(attended, axis=-1, keepdims=True)
    centered = attended - row_mean
    variance = jnp.mean(centered * centered, axis=-1, keepdims=True)
    inv_std = lax.rsqrt(variance + norm_eps)
    normed = centered * inv_std
    mixed_out = (normed * gate_f).astype(jnp.bfloat16)
    onehot = (requests[0][:, None] == jnp.arange(REQS, dtype=jnp.int32)[None, :]).astype(
        jnp.float32
    )
    live_f = is_live.astype(jnp.float32)
    inv_prop = jnp.where(is_live, 1.0 / propensity[0], 0.0)
    inv_sum, live_count = lax.psum(
        (jnp.sum(onehot * inv_prop[:, None], axis=0), jnp.sum(onehot * live_f[:, None], axis=0)),
        "ctx",
    )
    full_w = lax.all_gather(w_out, "ctx", axis=1, tiled=True)
    item_f = item_emb[0].astype(jnp.float32)
    item_proj = lax.dot_general(
        item_emb[0], full_w, (((1,), (1,)), ((), ())), preferred_element_type=jnp.float32
    )
    logits = jnp.sum(mixed_out.astype(jnp.float32) * item_proj, axis=-1)
    ratio = jnp.where(live_count > 0, live_count / jnp.where(live_count > 0, inv_sum, 1.0), 0.0)
    event_weight = inv_prop * jnp.sum(onehot * ratio[None, :], axis=-1)
    grad_logits = event_weight * (jax.nn.sigmoid(logits) - labels[0].astype(jnp.float32))
    grad_proj = (grad_logits[:, None] * item_f).astype(jnp.bfloat16)
    whole_grad = lax.dot_general(
        mixed_out, grad_proj, (((0,), (0,)), ((), ())), preferred_element_type=jnp.float32
    )
    partial_grad = lax.psum_scatter(whole_grad, "user", scatter_dimension=1, tiled=True)
    grad_w = lax.psum_scatter(partial_grad, "ctx", scatter_dimension=0, tiled=True)
    grad_mixed = grad_logits[:, None] * item_proj
    grad_gate = grad_mixed * normed
    grad_normed = grad_mixed * gate_f
    grad_attn = (
        grad_normed
        - jnp.mean(grad_normed, axis=-1, keepdims=True)
        - normed * jnp.mean(grad_normed * normed, axis=-1, keepdims=True)
    ) * inv_std
    grad_attn = grad_attn.astype(jnp.bfloat16)
    grad_attn_h = split_heads(grad_attn)
    key_piece = lax.all_gather(own_key, "ctx", axis=0, tiled=True)
    value_piece = lax.all_gather(own_value, "ctx", axis=0, tiled=True)
    piece_len = key_piece.shape[0]
    key_pos = jnp.arange(piece_len, dtype=jnp.int32)
    key_piece_h = split_heads(key_piece)
    scores = (
        jnp.einsum("qhd,khd->hqk", query_h, key_piece_h, preferred_element_type=jnp.float32)
        * score_factor
    )
    allowed = (key_pos[None, :] <= own_pos[:, None]) & (key_pos[None, :] < hist_len)
    grad_weights = jnp.einsum(
        "qhd,khd->hqk", grad_attn_h, split_heads(value_piece), preferred_element_type=jnp.float32
    )
    grad_scores = (
        jnp.where(allowed[None], grad_weights * silu_slope(scores), 0.0) / seq_len
    ).astype(jnp.bfloat16)
    added = (
        jnp.einsum("hqk,khd->qhd", grad_scores, key_piece_h, preferred_element_type=jnp.float32)
        * score_factor
    )
    grad_query = added.reshape(row_count, feat_width)
    query_piece = lax.all_gather(own_query, "ctx", axis=0, tiled=True)
    grad_piece = lax.all_gather(grad_attn, "ctx", axis=0, tiled=True)
    piece_len = query_piece.shape[0]
    query_pos = jnp.arange(piece_len, dtype=jnp.int32)
    query_piece_h = split_heads(query_piece)
    grad_piece_h = split_heads(grad_piece)
    scores = (
        jnp.einsum("qhd,khd->hqk", query_piece_h, key_h, preferred_element_type=jnp.float32)
        * score_factor
    )
    allowed = (own_pos[None, :] <= query_pos[:, None]) & (own_pos[None, :] < hist_len)
    weights = (jnp.where(allowed[None], jax.nn.silu(scores), 0.0) / seq_len).astype(jnp.bfloat16)
    grad_weights = jnp.einsum(
        "qhd,khd->hqk", grad_piece_h, value_h, preferred_element_type=jnp.float32
    )
    grad_scores = (
        jnp.where(allowed[None], grad_weights * silu_slope(scores), 0.0) / seq_len
    ).astype(jnp.bfloat16)
    added_key = (
        jnp.einsum("hqk,qhd->khd", grad_scores, query_piece_h, preferred_element_type=jnp.float32)
        * score_factor
    )
    added_value = jnp.einsum(
        "hqk,qhd->khd", weights, grad_piece_h, preferred_element_type=jnp.float32
    )
    grad_key = added_key.reshape(row_count, feat_width)
    grad_value = added_value.reshape(row_count, feat_width)
    return (grad_query[None], grad_key[None], grad_value[None], grad_gate[None], grad_w)


MESH = pl.DeviceIdType.MESH
F32 = jnp.float32
BF16 = jnp.bfloat16


def dot_nn(a, b):
    return lax.dot_general(a, b, (((1,), (0,)), ((), ())), preferred_element_type=F32)


def dot_nt(a, b):
    return lax.dot_general(a, b, (((1,), (1,)), ((), ())), preferred_element_type=F32)


def dot_tn(a, b):
    return lax.dot_general(a, b, (((0,), (0,)), ((), ())), preferred_element_type=F32)


def sigmoid(values):
    return 0.5 * jnp.tanh(0.5 * values) + 0.5


def head(h):
    return slice(h * HEAD_DIM, (h + 1) * HEAD_DIM)


def fused_kernel(
    users,
    len_ref, q_ref, k_ref, v_ref, gate_ref, item_ref, lab_ref, prop_ref, req_ref, w_ref,
    dq_ref, dk_ref, dv_ref, dgate_ref, dw_ref,
    ok, ov, oq, oda, wbuf, stat_out, stat_in,
    wt, sl, wt_x, sl_x, att, u, da, gw,
    r_core, s_y, r_y, s_z, r_z, fin, s_x, r_x,
    ks, kr, vs, vr, qs, qr, das, dar, wss, wsr, sts, str_, cs, cr, ys, yr, zs, zr, xs, xr,
):
    rows, feats = q_ref.shape
    width = item_ref.shape[1]
    half_w = width // 2
    seq_len = 2 * rows
    nz = users // 4
    cols = feats // 2
    factor = 1.0 / math.sqrt(HEAD_DIM)
    ctx = lax.axis_index("ctx")
    user = lax.axis_index("user")
    core = lax.rem(user, 2)
    yy = lax.rem(lax.div(user, 2), 2)
    zz = lax.div(user, 4)
    quarter = lax.rem(user, 4)
    offset = ctx * rows
    x_peer = (1 - ctx, user)
    c_peer = (ctx, user + 1 - 2 * core)
    y_peer = (ctx, user + 2 - 4 * yy)
    d_peer = (ctx, user + 3 - 2 * core - 4 * yy)
    z_peers = [(ctx, quarter + 4 * lax.rem(zz + step, nz)) for step in range(1, nz)]

    def remote(source, target, send_sem, recv_sem, device):
        return pltpu.make_async_remote_copy(
            src_ref=source, dst_ref=target, send_sem=send_sem, recv_sem=recv_sem,
            device_id=device, device_id_type=MESH,
        )

    hist_len = len_ref[0]
    reqs = req_ref[...]
    onehot = (lax.broadcasted_iota(jnp.int32, (REQS, rows), 0) == reqs).astype(F32)
    live = offset + lax.broadcasted_iota(jnp.int32, (1, rows), 1) < hist_len
    inv_prop = jnp.where(live, 1.0 / prop_ref[...], 0.0)
    own_inv = jnp.sum(onehot * inv_prop, axis=1, keepdims=True)
    own_live = jnp.sum(onehot * jnp.where(live, 1.0, 0.0), axis=1, keepdims=True)
    lane = lax.broadcasted_iota(jnp.int32, (REQS, 128), 1)
    stat_out[...] = jnp.where(lane == 0, own_inv, own_live)

    peers = [x_peer, c_peer, y_peer, d_peer] + z_peers
    barrier = pltpu.get_barrier_semaphore()
    for peer in peers:
        pl.semaphore_signal(barrier, inc=1, device_id=peer, device_id_type=MESH)
    pl.semaphore_wait(barrier, len(peers))

    stat_copy = remote(stat_out, stat_in, sts, str_, x_peer)
    w_part = feats // 4
    w_rows = pl.ds(pl.multiple_of(quarter * w_part, w_part), w_part)
    w_copy = remote(w_ref.at[w_rows], wbuf.at[quarter], wss.at[0], wsr.at[0], x_peer)
    w_spread = [
        remote(wbuf.at[quarter], wbuf.at[quarter], wss.at[i], wsr.at[i], peer)
        for i, peer in ((1, c_peer), (2, y_peer), (3, d_peer))
    ]
    k_copy = [remote(k_ref.at[:, head(h)], ok.at[h], ks.at[h], kr.at[h], x_peer) for h in range(HEADS)]
    v_copy = [remote(v_ref.at[:, head(h)], ov.at[h], vs.at[h], vr.at[h], x_peer) for h in range(HEADS)]
    q_copy = [remote(q_ref.at[:, head(h)], oq.at[h], qs.at[h], qr.at[h], x_peer) for h in range(HEADS)]
    da_copy = [remote(da.at[h], oda.at[h], das.at[h], dar.at[h], x_peer) for h in range(HEADS)]

    stat_copy.start()
    w_copy.start()

    @pl.when(ctx == 0)
    def _():
        for h in range(HEADS):
            k_copy[h].start()
            v_copy[h].start()

    @pl.when(ctx == 1)
    def _():
        for h in range(HEADS):
            q_copy[h].start()

    def gates(scores, allowed):
        s = scores * factor
        sig = sigmoid(s)
        weight = jnp.where(allowed, s * sig, 0.0) * (1.0 / seq_len)
        slope = jnp.where(allowed, sig * (1.0 + s * (1.0 - sig)), 0.0) * (1.0 / seq_len)
        return weight.astype(BF16), slope

    row_i = lax.broadcasted_iota(jnp.int32, (rows, rows), 0)
    col_i = lax.broadcasted_iota(jnp.int32, (rows, rows), 1)
    allowed = (col_i <= row_i) & (offset + col_i < hist_len)
    for h in range(HEADS):
        weight, slope = gates(dot_nt(q_ref[:, head(h)], k_ref[:, head(h)]), allowed)
        wt[h] = weight
        sl[h] = slope
        att[:, head(h)] = dot_nn(weight, v_ref[:, head(h)])

    own_cols = pl.ds(pl.multiple_of(ctx * half_w, half_w), half_w)
    other_cols = pl.ds(pl.multiple_of((1 - ctx) * half_w, half_w), half_w)
    w_copy.wait_recv()
    for copy in w_spread:
        copy.start()
    u[...] = dot_nt(item_ref[:, own_cols], w_ref[...])

    @pl.when(ctx == 1)
    def _():
        seen = lax.broadcasted_iota(jnp.int32, (rows, rows), 1) < hist_len
        for h in range(HEADS):
            k_copy[h].wait_recv()
            weight, slope = gates(dot_nt(q_ref[:, head(h)], ok[h]), seen)
            sl_x[h] = slope
            v_copy[h].wait_recv()
            att[:, head(h)] += dot_nn(weight, ov[h])

    for copy in w_spread:
        copy.wait_recv()
    for part in range(4):
        part_cols = slice(part * w_part, (part + 1) * w_part)
        u[:, part_cols] += dot_nt(item_ref[:, other_cols], wbuf[part])

    attended = att[...]
    centered = attended - jnp.mean(attended, axis=-1, keepdims=True)
    inv_std = lax.rsqrt(jnp.mean(centered * centered, axis=-1, keepdims=True) + norm_eps)
    normed = centered * inv_std
    gate_f = gate_ref[...].astype(F32)
    mixed_out = (normed * gate_f).astype(BF16)
    item_proj = u[...]
    logits = jnp.sum(mixed_out.astype(F32) * item_proj, axis=-1, keepdims=True)

    stat_copy.wait_recv()
    both = stat_out[...] + stat_in[...]
    inv_sum, live_count = both[:, 0:1], both[:, 1:2]
    some = live_count > 0
    ratio = jnp.where(some, live_count / jnp.where(some, inv_sum, 1.0), 0.0)
    event_weight = inv_prop * jnp.sum(onehot * ratio, axis=0, keepdims=True)
    eye = row_i == col_i
    weight_col = jnp.sum(jnp.where(eye, event_weight, 0.0), axis=1, keepdims=True)
    label_col = jnp.sum(jnp.where(eye, lab_ref[...].astype(F32), 0.0), axis=1, keepdims=True)
    grad_logits = weight_col * (jax.nn.sigmoid(logits) - label_col)
    grad_mixed = grad_logits * item_proj
    dgate_ref[...] = grad_mixed * normed
    grad_normed = grad_mixed * gate_f
    grad_attn = (
        grad_normed
        - jnp.mean(grad_normed, axis=-1, keepdims=True)
        - normed * jnp.mean(grad_normed * normed, axis=-1, keepdims=True)
    ) * inv_std
    for h in range(HEADS):
        da[h] = grad_attn[:, head(h)].astype(BF16)

    @pl.when(ctx == 1)
    def _():
        for h in range(HEADS):
            da_copy[h].start()

    per_user = width // users
    for j in range(users // 2):
        chunk_cols = slice(j * 2 * per_user, (j + 1) * 2 * per_user)
        grad_proj = (grad_logits * item_ref[:, chunk_cols].astype(F32)).astype(BF16)
        chunk = dot_tn(grad_proj, mixed_out).astype(BF16)
        for c in range(2):
            for half in range(2):
                gw[c, half, j % 2, j // 2] = chunk[
                    c * per_user : (c + 1) * per_user, half * cols : (half + 1) * cols
                ]
    halves = [1 - ctx, ctx]
    c_copy = [remote(gw.at[1 - core, halves[o]], r_core.at[o], cs.at[o], cr.at[o], c_peer) for o in range(2)]
    y_copy = [remote(s_y.at[o], r_y.at[o], ys.at[o], yr.at[o], y_peer) for o in range(2)]
    z_copy = [
        [
            remote(
                s_z.at[o, lax.rem(zz + i + 1, nz)], r_z.at[o, i], zs.at[o, i], zr.at[o, i], z_peers[i]
            )
            for i in range(nz - 1)
        ]
        for o in range(2)
    ]
    x_copy = remote(s_x, r_x, xs, xr, x_peer)
    for o in range(2):
        c_copy[o].start()

    def after_core(o):
        c_copy[o].wait_recv()
        s_y[o] = (gw[core, halves[o], 1 - yy].astype(F32) + r_core[o, 1 - yy].astype(F32)).astype(BF16)
        y_copy[o].start()

    def after_y(o):
        y_copy[o].wait_recv()
        mine = gw[core, halves[o], yy].astype(F32) + r_core[o, yy].astype(F32)
        s_z[o] = (mine + r_y[o].astype(F32)).astype(BF16)
        for copy in z_copy[o]:
            copy.start()

    def after_z(o):
        total = gw[core, halves[o], yy, zz].astype(F32) + r_core[o, yy, zz].astype(F32)
        total += r_y[o, zz].astype(F32)
        for i in range(nz - 1):
            z_copy[o][i].wait_recv()
            total += r_z[o, i].astype(F32)
        if o == 0:
            s_x[...] = total.astype(BF16)
            x_copy.start()
        else:
            fin[...] = total

    def backward(h):
        grad_scores = (dot_nt(da[h], v_ref[:, head(h)]) * sl[h]).astype(BF16)
        dq_ref[:, head(h)] = dot_nn(grad_scores, k_ref[:, head(h)]) * factor
        dk_ref[:, head(h)] = dot_tn(grad_scores, q_ref[:, head(h)]) * factor
        dv_ref[:, head(h)] = dot_tn(wt[h], da[h])

    def cross_query(h):
        grad_scores = (dot_nt(da[h], ov[h]) * sl_x[h]).astype(BF16)
        dq_ref[:, head(h)] += dot_nn(grad_scores, ok[h]) * factor

    def cross_scores(h):
        q_copy[h].wait_recv()
        seen = lax.broadcasted_iota(jnp.int32, (rows, rows), 1) < hist_len
        weight, slope = gates(dot_nt(oq[h], k_ref[:, head(h)]), seen)
        wt_x[h] = weight
        sl_x[h] = slope

    def cross_key(h):
        da_copy[h].wait_recv()
        grad_scores = (dot_nt(oda[h], v_ref[:, head(h)]) * sl_x[h]).astype(BF16)
        dk_ref[:, head(h)] += dot_tn(grad_scores, oq[h]) * factor
        dv_ref[:, head(h)] += dot_tn(wt_x[h], oda[h])

    backward(0)
    after_core(0)
    backward(1)
    after_core(1)
    backward(2)
    backward(3)
    after_y(0)

    @pl.when(ctx == 0)
    def _():
        for h in range(HEADS):
            cross_scores(h)

    @pl.when(ctx == 1)
    def _():
        for h in range(HEADS):
            cross_query(h)

    after_y(1)
    after_z(0)
    after_z(1)

    @pl.when(ctx == 0)
    def _():
        for h in range(HEADS):
            cross_key(h)
        for h in range(HEADS):
            k_copy[h].wait_send()
            v_copy[h].wait_send()

    @pl.when(ctx == 1)
    def _():
        for h in range(HEADS):
            q_copy[h].wait_send()
            da_copy[h].wait_send()

    x_copy.wait_recv()
    dw_ref[...] = fin[...] + r_x[...].astype(F32)
    for copy in [stat_copy, w_copy, x_copy] + w_spread + c_copy + y_copy + z_copy[0] + z_copy[1]:
        copy.wait_send()


def fused(
    users, queries, key_rows, value_rows, gate_rows, item_emb, labels, propensity, requests, lengths, w_out
):
    _, rows, feats = queries.shape
    width = item_emb.shape[2]
    per_user = width // users
    nz = users // 4
    cols = feats // 2
    dma = pltpu.SemaphoreType.DMA
    block = (HEADS, rows, HEAD_DIM)
    square = (HEADS, rows, rows)
    vmem = pl.BlockSpec(memory_space=pltpu.VMEM)
    out = jax.ShapeDtypeStruct((rows, feats), F32)
    results = pl.pallas_call(
        functools.partial(fused_kernel, users),
        out_shape=[out, out, out, out, jax.ShapeDtypeStruct((per_user, cols), F32)],
        in_specs=[pl.BlockSpec(memory_space=pltpu.SMEM)] + [vmem] * 9,
        out_specs=[vmem] * 5,
        scratch_shapes=[
            pltpu.VMEM(block, BF16),
            pltpu.VMEM(block, BF16),
            pltpu.VMEM(block, BF16),
            pltpu.VMEM(block, BF16),
            pltpu.VMEM((4, feats // 4, width // 2), BF16),
            pltpu.VMEM((REQS, 128), F32),
            pltpu.VMEM((REQS, 128), F32),
            pltpu.VMEM(square, BF16),
            pltpu.VMEM(square, F32),
            pltpu.VMEM(square, BF16),
            pltpu.VMEM(square, F32),
            pltpu.VMEM((rows, feats), F32),
            pltpu.VMEM((rows, feats), F32),
            pltpu.VMEM(block, BF16),
            pltpu.VMEM((2, 2, 2, nz, per_user, cols), BF16),
            pltpu.VMEM((2, 2, nz, per_user, cols), BF16),
            pltpu.VMEM((2, nz, per_user, cols), BF16),
            pltpu.VMEM((2, nz, per_user, cols), BF16),
            pltpu.VMEM((2, nz, per_user, cols), BF16),
            pltpu.VMEM((2, nz - 1, per_user, cols), BF16),
            pltpu.VMEM((per_user, cols), F32),
            pltpu.VMEM((per_user, cols), BF16),
            pltpu.VMEM((per_user, cols), BF16),
        ]
        + [dma((HEADS,))] * 8
        + [dma((4,))] * 2
        + [dma] * 2
        + [dma((2,))] * 4
        + [dma((2, nz - 1))] * 2
        + [dma] * 2,
        compiler_params=pltpu.CompilerParams(
            collective_id=0, has_side_effects=True, vmem_limit_bytes=48 * 1024 * 1024
        ),
        cost_estimate=pl.CostEstimate(
            flops=4 * 10**9, bytes_accessed=5 * 10**6, transcendentals=10**6
        ),
    )(
        lengths, queries[0], key_rows[0], value_rows[0], gate_rows[0], item_emb[0],
        labels, propensity, requests, w_out,
    )
    dq, dk, dv, dgate, dw = results
    return dq[None], dk[None], dv[None], dgate[None], dw.T


def solution(mesh):
    in_specs = (
        P("user", "ctx", None),
        P("user", "ctx", None),
        P("user", "ctx", None),
        P("user", "ctx", None),
        P("user", "ctx", None),
        P("user", "ctx"),
        P("user", "ctx"),
        P("user", "ctx"),
        P("user"),
        P(None, "ctx"),
    )
    out_specs = (
        P("user", "ctx", None),
        P("user", "ctx", None),
        P("user", "ctx", None),
        P("user", "ctx", None),
        P("ctx", "user"),
    )
    users = mesh.shape["user"]
    two_blocks = mesh.shape["ctx"] == 2 and users % 4 == 0
    step = functools.partial(fused, users) if two_blocks else local
    return jax.shard_map(step, mesh=mesh, in_specs=in_specs, out_specs=out_specs, check_vma=False)
```

```python
import functools
import math

import jax
import jax.numpy as jnp
from jax import lax
from jax.experimental import pallas as pl
from jax.experimental.pallas import tpu as pltpu
from jax.sharding import PartitionSpec as P

HEADS = 4
HEAD_DIM = 128
REQS = 64


norm_eps = 1e-06


def silu_slope(values):
    sigmoid_v = jax.nn.sigmoid(values)
    return sigmoid_v * (1.0 + values * (1.0 - sigmoid_v))


def split_heads(block):
    return block.reshape(block.shape[0], HEADS, HEAD_DIM)


def local(
    queries, key_rows, value_rows, gate_rows, item_emb, labels, propensity, requests, lengths, w_out
):
    row_count = queries.shape[1]
    feat_width = queries.shape[2]
    groups = lax.axis_size("ctx")
    seq_len = row_count * groups
    offset = lax.axis_index("ctx") * row_count
    score_factor = 1.0 / math.sqrt(HEAD_DIM)
    own_query = queries[0]
    own_key = key_rows[0]
    own_value = value_rows[0]
    query_h = split_heads(own_query)
    key_h = split_heads(own_key)
    value_h = split_heads(own_value)
    gate_f = gate_rows[0].astype(jnp.float32)
    hist_len = lengths[0]
    own_pos = offset + jnp.arange(row_count, dtype=jnp.int32)
    is_live = own_pos < hist_len
    key_piece = lax.all_gather(own_key, "ctx", axis=0, tiled=True)
    value_piece = lax.all_gather(own_value, "ctx", axis=0, tiled=True)
    piece_len = key_piece.shape[0]
    key_pos = jnp.arange(piece_len, dtype=jnp.int32)
    scores = (
        jnp.einsum(
            "qhd,khd->hqk", query_h, split_heads(key_piece), preferred_element_type=jnp.float32
        )
        * score_factor
    )
    allowed = (key_pos[None, :] <= own_pos[:, None]) & (key_pos[None, :] < hist_len)
    weights = (jnp.where(allowed[None], jax.nn.silu(scores), 0.0) / seq_len).astype(jnp.bfloat16)
    added = jnp.einsum(
        "hqk,khd->qhd", weights, split_heads(value_piece), preferred_element_type=jnp.float32
    )
    attended = added.reshape(row_count, feat_width)
    row_mean = jnp.mean(attended, axis=-1, keepdims=True)
    centered = attended - row_mean
    variance = jnp.mean(centered * centered, axis=-1, keepdims=True)
    inv_std = lax.rsqrt(variance + norm_eps)
    normed = centered * inv_std
    mixed_out = (normed * gate_f).astype(jnp.bfloat16)
    onehot = (requests[0][:, None] == jnp.arange(REQS, dtype=jnp.int32)[None, :]).astype(
        jnp.float32
    )
    live_f = is_live.astype(jnp.float32)
    inv_prop = jnp.where(is_live, 1.0 / propensity[0], 0.0)
    inv_sum, live_count = lax.psum(
        (jnp.sum(onehot * inv_prop[:, None], axis=0), jnp.sum(onehot * live_f[:, None], axis=0)),
        "ctx",
    )
    full_w = lax.all_gather(w_out, "ctx", axis=1, tiled=True)
    item_f = item_emb[0].astype(jnp.float32)
    item_proj = lax.dot_general(
        item_emb[0], full_w, (((1,), (1,)), ((), ())), preferred_element_type=jnp.float32
    )
    logits = jnp.sum(mixed_out.astype(jnp.float32) * item_proj, axis=-1)
    ratio = jnp.where(live_count > 0, live_count / jnp.where(live_count > 0, inv_sum, 1.0), 0.0)
    event_weight = inv_prop * jnp.sum(onehot * ratio[None, :], axis=-1)
    grad_logits = event_weight * (jax.nn.sigmoid(logits) - labels[0].astype(jnp.float32))
    grad_proj = (grad_logits[:, None] * item_f).astype(jnp.bfloat16)
    whole_grad = lax.dot_general(
        mixed_out, grad_proj, (((0,), (0,)), ((), ())), preferred_element_type=jnp.float32
    )
    partial_grad = lax.psum_scatter(whole_grad, "user", scatter_dimension=1, tiled=True)
    grad_w = lax.psum_scatter(partial_grad, "ctx", scatter_dimension=0, tiled=True)
    grad_mixed = grad_logits[:, None] * item_proj
    grad_gate = grad_mixed * normed
    grad_normed = grad_mixed * gate_f
    grad_attn = (
        grad_normed
        - jnp.mean(grad_normed, axis=-1, keepdims=True)
        - normed * jnp.mean(grad_normed * normed, axis=-1, keepdims=True)
    ) * inv_std
    grad_attn = grad_attn.astype(jnp.bfloat16)
    grad_attn_h = split_heads(grad_attn)
    key_piece = lax.all_gather(own_key, "ctx", axis=0, tiled=True)
    value_piece = lax.all_gather(own_value, "ctx", axis=0, tiled=True)
    piece_len = key_piece.shape[0]
    key_pos = jnp.arange(piece_len, dtype=jnp.int32)
    key_piece_h = split_heads(key_piece)
    scores = (
        jnp.einsum("qhd,khd->hqk", query_h, key_piece_h, preferred_element_type=jnp.float32)
        * score_factor
    )
    allowed = (key_pos[None, :] <= own_pos[:, None]) & (key_pos[None, :] < hist_len)
    grad_weights = jnp.einsum(
        "qhd,khd->hqk", grad_attn_h, split_heads(value_piece), preferred_element_type=jnp.float32
    )
    grad_scores = (
        jnp.where(allowed[None], grad_weights * silu_slope(scores), 0.0) / seq_len
    ).astype(jnp.bfloat16)
    added = (
        jnp.einsum("hqk,khd->qhd", grad_scores, key_piece_h, preferred_element_type=jnp.float32)
        * score_factor
    )
    grad_query = added.reshape(row_count, feat_width)
    query_piece = lax.all_gather(own_query, "ctx", axis=0, tiled=True)
    grad_piece = lax.all_gather(grad_attn, "ctx", axis=0, tiled=True)
    piece_len = query_piece.shape[0]
    query_pos = jnp.arange(piece_len, dtype=jnp.int32)
    query_piece_h = split_heads(query_piece)
    grad_piece_h = split_heads(grad_piece)
    scores = (
        jnp.einsum("qhd,khd->hqk", query_piece_h, key_h, preferred_element_type=jnp.float32)
        * score_factor
    )
    allowed = (own_pos[None, :] <= query_pos[:, None]) & (own_pos[None, :] < hist_len)
    weights = (jnp.where(allowed[None], jax.nn.silu(scores), 0.0) / seq_len).astype(jnp.bfloat16)
    grad_weights = jnp.einsum(
        "qhd,khd->hqk", grad_piece_h, value_h, preferred_element_type=jnp.float32
    )
    grad_scores = (
        jnp.where(allowed[None], grad_weights * silu_slope(scores), 0.0) / seq_len
    ).astype(jnp.bfloat16)
    added_key = (
        jnp.einsum("hqk,qhd->khd", grad_scores, query_piece_h, preferred_element_type=jnp.float32)
        * score_factor
    )
    added_value = jnp.einsum(
        "hqk,qhd->khd", weights, grad_piece_h, preferred_element_type=jnp.float32
    )
    grad_key = added_key.reshape(row_count, feat_width)
    grad_value = added_value.reshape(row_count, feat_width)
    return (grad_query[None], grad_key[None], grad_value[None], grad_gate[None], grad_w)


MESH = pl.DeviceIdType.MESH
F32 = jnp.float32
BF16 = jnp.bfloat16
NEAR = 2


def dot_nn(a, b):
    return lax.dot_general(a, b, (((1,), (0,)), ((), ())), preferred_element_type=F32)


def dot_nt(a, b):
    return lax.dot_general(a, b, (((1,), (1,)), ((), ())), preferred_element_type=F32)


def dot_tn(a, b):
    return lax.dot_general(a, b, (((0,), (0,)), ((), ())), preferred_element_type=F32)


def sigmoid(values):
    return 0.5 * jnp.tanh(0.5 * values) + 0.5


def head(h):
    return slice(h * HEAD_DIM, (h + 1) * HEAD_DIM)


def fused_kernel(
    users,
    len_ref, q_hbm, k_hbm, v_hbm, gate_hbm, item_hbm, lab_hbm, prop_hbm, req_hbm, w_hbm,
    dq_ref, dk_ref, dv_ref, dgate_ref, dw_ref,
    q_ref, k_ref, v_ref, gate_ref, item_ref, lab_ref, prop_ref, req_ref, w_ref, load,
    ok, ov, oq, oda, wbuf, stat_out, stat_in, part_out, part_in, mixed, grad_proj_t,
    wt, sl, wt_x, sl_x, att, u, da, gw,
    r_core, s_y, r_y, s_z, r_z, fin, s_x, r_x,
    ks, kr, vs, vr, qs, qr, das, dar, wss, wsr, sts, str_, ps, pr, cs, cr, ys, yr, zs, zr, xs, xr,
):
    rows, feats = q_ref.shape
    pairs = (
        (q_hbm, q_ref), (k_hbm, k_ref), (v_hbm, v_ref), (w_hbm, w_ref), (item_hbm, item_ref),
        (gate_hbm, gate_ref), (prop_hbm, prop_ref), (req_hbm, req_ref), (lab_hbm, lab_ref),
    )
    loads = [pltpu.make_async_copy(a, b, load.at[i]) for i, (a, b) in enumerate(pairs)]
    for copy in loads:
        copy.start()
    width = item_ref.shape[1]
    half_w = width // 2
    seq_len = 2 * rows
    nz = users // 4
    cols = feats // 2
    factor = 1.0 / math.sqrt(HEAD_DIM)
    ctx = lax.axis_index("ctx")
    user = lax.axis_index("user")
    core = lax.rem(user, 2)
    yy = lax.rem(lax.div(user, 2), 2)
    zz = lax.div(user, 4)
    quarter = lax.rem(user, 4)
    offset = ctx * rows
    x_peer = (1 - ctx, user)
    c_peer = (ctx, user + 1 - 2 * core)
    y_peer = (ctx, user + 2 - 4 * yy)
    pair_peer = (ctx, quarter + 4 * (zz + 1 - 2 * lax.rem(zz, 2)))
    z_peers = [(ctx, quarter + 4 * lax.rem(zz + step, nz)) for step in range(1, nz)]

    def remote(source, target, send_sem, recv_sem, device):
        return pltpu.make_async_remote_copy(
            src_ref=source, dst_ref=target, send_sem=send_sem, recv_sem=recv_sem,
            device_id=device, device_id_type=MESH,
        )

    peers = [x_peer, c_peer, y_peer] + z_peers
    barrier = pltpu.get_barrier_semaphore()
    for peer in peers:
        pl.semaphore_signal(barrier, inc=1, device_id=peer, device_id_type=MESH)
    pl.semaphore_wait(barrier, len(peers))

    stat_copy = remote(stat_out, stat_in, sts, str_, x_peer)
    w_part = feats // 4
    w_slice = w_part // 2
    w_at = pl.multiple_of(lax.rem(zz, 2) * w_slice, w_slice)
    w_rows = pl.ds(pl.multiple_of(quarter * w_part, w_part) + w_at, w_slice)
    w_piece = wbuf.at[quarter, pl.ds(w_at, w_slice)]
    far = quarter + 2 - 4 * yy
    w_copy = remote(w_hbm.at[w_rows], w_piece, wss.at[0], wsr.at[0], x_peer)
    w_pair = remote(w_piece, w_piece, wss.at[1], wsr.at[1], pair_peer)
    w_core = remote(wbuf.at[quarter], wbuf.at[quarter], wss.at[2], wsr.at[2], c_peer)
    w_y = remote(wbuf.at[quarter], wbuf.at[quarter], wss.at[3], wsr.at[3], y_peer)
    w_far = remote(wbuf.at[far], wbuf.at[far], wss.at[4], wsr.at[4], c_peer)
    w_all = [w_copy, w_pair, w_core, w_y, w_far]
    k_copy = [remote(k_hbm.at[:, head(h)], ok.at[h], ks.at[h], kr.at[h], x_peer) for h in range(HEADS)]
    v_copy = [remote(v_hbm.at[:, head(h)], ov.at[h], vs.at[h], vr.at[h], x_peer) for h in range(HEADS)]
    q_copy = [remote(q_hbm.at[:, head(h)], oq.at[h], qs.at[h], qr.at[h], x_peer) for h in range(HEADS)]
    da_copy = [remote(da.at[h], oda.at[h], das.at[h], dar.at[h], x_peer) for h in range(HEADS)]

    part_copy = [remote(part_out.at[i], part_in.at[i], ps.at[i], pr.at[i], x_peer) for i in range(HEADS - NEAR)]
    w_copy.start()

    @pl.when(ctx == 0)
    def _():
        for h in range(NEAR):
            k_copy[h].start()
            v_copy[h].start()

    @pl.when(ctx == 1)
    def _():
        for h in list(range(NEAR, HEADS)) + list(range(NEAR)):
            q_copy[h].start()

    for copy in loads:
        copy.wait()
    hist_len = len_ref[0]
    reqs = req_ref[...]
    onehot = (lax.broadcasted_iota(jnp.int32, (REQS, rows), 0) == reqs).astype(F32)
    live = offset + lax.broadcasted_iota(jnp.int32, (1, rows), 1) < hist_len
    inv_prop = jnp.where(live, 1.0 / prop_ref[...], 0.0)
    live_f = jnp.where(live, 1.0, 0.0)
    stat_out[0:1] = reqs.astype(F32)
    stat_out[1:2] = inv_prop
    stat_out[2:3] = live_f
    stat_out[3:8] = jnp.zeros((5, rows), F32)

    stat_copy.start()

    def gates(scores, allowed):
        s = scores * factor
        sig = sigmoid(s)
        weight = jnp.where(allowed, s * sig, 0.0) * (1.0 / seq_len)
        slope = jnp.where(allowed, sig * (1.0 + s * (1.0 - sig)), 0.0) * (1.0 / seq_len)
        return weight.astype(BF16), slope

    row_i = lax.broadcasted_iota(jnp.int32, (rows, rows), 0)
    col_i = lax.broadcasted_iota(jnp.int32, (rows, rows), 1)
    allowed = (col_i <= row_i) & (offset + col_i < hist_len)
    for h in range(HEADS):
        weight, slope = gates(dot_nt(q_ref[:, head(h)], k_ref[:, head(h)]), allowed)
        wt[h] = weight
        sl[h] = slope
        att[:, head(h)] = dot_nn(weight, v_ref[:, head(h)])

    own_cols = pl.ds(pl.multiple_of(ctx * half_w, half_w), half_w)
    other_cols = pl.ds(pl.multiple_of((1 - ctx) * half_w, half_w), half_w)
    seen = lax.broadcasted_iota(jnp.int32, (rows, rows), 1) < hist_len

    def cross_scores(h):
        q_copy[h].wait_recv()
        weight, slope = gates(dot_nt(oq[h], k_ref[:, head(h)]), seen)
        wt_x[h] = weight
        sl_x[h] = slope

    w_copy.wait_recv()
    w_pair.start()

    @pl.when(ctx == 0)
    def _():
        for h in range(NEAR, HEADS):
            cross_scores(h)
            part_out[h - NEAR] = dot_nn(wt_x[h], v_ref[:, head(h)]).astype(BF16)
            part_copy[h - NEAR].start()
        for h in range(NEAR, HEADS):
            k_copy[h].start()
            v_copy[h].start()

    w_pair.wait_recv()
    w_y.start()
    w_core.start()
    u[...] = dot_nt(item_ref[:, own_cols], w_ref[...])

    @pl.when(ctx == 1)
    def _():
        for h in range(NEAR):
            k_copy[h].wait_recv()
            weight, slope = gates(dot_nt(q_ref[:, head(h)], ok[h]), seen)
            sl_x[h] = slope
            v_copy[h].wait_recv()
            att[:, head(h)] += dot_nn(weight, ov[h])

    w_y.wait_recv()
    w_far.start()

    @pl.when(ctx == 1)
    def _():
        for h in range(NEAR, HEADS):
            part_copy[h - NEAR].wait_recv()
            att[:, head(h)] += part_in[h - NEAR].astype(F32)

    w_core.wait_recv()
    w_far.wait_recv()
    for part in range(4):
        part_cols = slice(part * w_part, (part + 1) * w_part)
        u[:, part_cols] += dot_nt(item_ref[:, other_cols], wbuf[part])

    attended = att[...]
    centered = attended - jnp.mean(attended, axis=-1, keepdims=True)
    inv_std = lax.rsqrt(jnp.mean(centered * centered, axis=-1, keepdims=True) + norm_eps)
    normed = centered * inv_std
    gate_f = gate_ref[...].astype(F32)
    mixed_out = (normed * gate_f).astype(BF16)
    item_proj = u[...]
    logits = jnp.sum(mixed_out.astype(F32) * item_proj, axis=-1, keepdims=True)

    stat_copy.wait_recv()
    onehot_x = (
        lax.broadcasted_iota(jnp.int32, (REQS, rows), 0) == stat_in[0:1].astype(jnp.int32)
    ).astype(F32)
    inv_sum = jnp.sum(onehot * inv_prop + onehot_x * stat_in[1:2], axis=1, keepdims=True)
    live_count = jnp.sum(onehot * live_f + onehot_x * stat_in[2:3], axis=1, keepdims=True)
    some = live_count > 0
    ratio = jnp.where(some, live_count / jnp.where(some, inv_sum, 1.0), 0.0)
    event_weight = inv_prop * jnp.sum(onehot * ratio, axis=0, keepdims=True)
    eye = row_i == col_i
    weight_col = jnp.sum(jnp.where(eye, event_weight, 0.0), axis=1, keepdims=True)
    label_col = jnp.sum(jnp.where(eye, lab_ref[...].astype(F32), 0.0), axis=1, keepdims=True)
    grad_logits = weight_col * (jax.nn.sigmoid(logits) - label_col)
    grad_mixed = grad_logits * item_proj
    dgate_ref[...] = grad_mixed * normed
    grad_normed = grad_mixed * gate_f
    grad_attn = (
        grad_normed
        - jnp.mean(grad_normed, axis=-1, keepdims=True)
        - normed * jnp.mean(grad_normed * normed, axis=-1, keepdims=True)
    ) * inv_std
    for h in range(HEADS):
        da[h] = grad_attn[:, head(h)].astype(BF16)

    @pl.when(ctx == 1)
    def _():
        for h in range(HEADS):
            da_copy[h].start()

    per_user = width // users
    for half in range(2):
        mixed[half] = mixed_out[:, half * cols : (half + 1) * cols]
    halves = [1 - ctx, ctx]
    c_copy = [remote(gw.at[1 - core, o], r_core.at[o], cs.at[o], cr.at[o], c_peer) for o in range(2)]
    y_copy = [remote(s_y.at[o], r_y.at[o], ys.at[o], yr.at[o], y_peer) for o in range(2)]
    z_copy = [
        [
            remote(
                s_z.at[o, lax.rem(zz + i + 1, nz)], r_z.at[o, i], zs.at[o, i], zr.at[o, i], z_peers[i]
            )
            for i in range(nz - 1)
        ]
        for o in range(2)
    ]
    x_copy = remote(s_x, r_x, xs, xr, x_peer)
    for o in range(2):
        for j in range(users // 2):
            if o == 0:
                chunk_cols = slice(j * 2 * per_user, (j + 1) * 2 * per_user)
                grad_proj = (grad_logits * item_ref[:, chunk_cols].astype(F32)).astype(BF16)
                grad_proj_t[j] = grad_proj.T
            chunk = dot_nn(grad_proj_t[j], mixed[halves[o]]).astype(BF16)
            for c in range(2):
                gw[c, o, j % 2, j // 2] = chunk[c * per_user : (c + 1) * per_user]
        c_copy[o].start()

    def after_core(o):
        c_copy[o].wait_recv()
        s_y[o] = (gw[core, o, 1 - yy].astype(F32) + r_core[o, 1 - yy].astype(F32)).astype(BF16)
        y_copy[o].start()

    def after_y(o):
        y_copy[o].wait_recv()
        mine = gw[core, o, yy].astype(F32) + r_core[o, yy].astype(F32)
        s_z[o] = (mine + r_y[o].astype(F32)).astype(BF16)
        for copy in z_copy[o]:
            copy.start()

    def after_z(o):
        total = gw[core, o, yy, zz].astype(F32) + r_core[o, yy, zz].astype(F32)
        total += r_y[o, zz].astype(F32)
        for i in range(nz - 1):
            z_copy[o][i].wait_recv()
            total += r_z[o, i].astype(F32)
        if o == 0:
            s_x[...] = total.astype(BF16)
            x_copy.start()
        else:
            fin[...] = total

    def backward(h):
        grad_scores = (dot_nt(da[h], v_ref[:, head(h)]) * sl[h]).astype(BF16)
        dq_ref[:, head(h)] = dot_nn(grad_scores, k_ref[:, head(h)]) * factor
        dk_ref[:, head(h)] = dot_tn(grad_scores, q_ref[:, head(h)]) * factor
        dv_ref[:, head(h)] = dot_tn(wt[h], da[h])

    def cross_query(h):
        grad_scores = (dot_nt(da[h], ov[h]) * sl_x[h]).astype(BF16)
        dq_ref[:, head(h)] += dot_nn(grad_scores, ok[h]) * factor

    def cross_key(h):
        da_copy[h].wait_recv()
        grad_scores = (dot_nt(oda[h], v_ref[:, head(h)]) * sl_x[h]).astype(BF16)
        dk_ref[:, head(h)] += dot_tn(grad_scores, oq[h]) * factor
        dv_ref[:, head(h)] += dot_tn(wt_x[h], oda[h])

    backward(0)
    after_core(0)
    backward(1)
    after_core(1)
    backward(2)
    backward(3)
    after_y(0)

    @pl.when(ctx == 0)
    def _():
        for h in range(NEAR):
            cross_scores(h)

    @pl.when(ctx == 1)
    def _():
        for h in range(NEAR, HEADS):
            k_copy[h].wait_recv()
            v_copy[h].wait_recv()
            sl_x[h] = gates(dot_nt(q_ref[:, head(h)], ok[h]), seen)[1]
        for h in range(HEADS):
            cross_query(h)

    after_y(1)
    after_z(0)
    after_z(1)

    @pl.when(ctx == 0)
    def _():
        for h in range(HEADS):
            cross_key(h)
        for h in range(HEADS):
            k_copy[h].wait_send()
            v_copy[h].wait_send()
        for copy in part_copy:
            copy.wait_send()

    @pl.when(ctx == 1)
    def _():
        for h in range(HEADS):
            q_copy[h].wait_send()
            da_copy[h].wait_send()

    x_copy.wait_recv()
    dw_ref[...] = fin[...] + r_x[...].astype(F32)
    for copy in [stat_copy, x_copy] + w_all + c_copy + y_copy + z_copy[0] + z_copy[1]:
        copy.wait_send()


def write_kernel(a, b, c, d, e, a_out, b_out, c_out, d_out, e_out, sems):
    copies = [
        pltpu.make_async_copy(src, dst, sems.at[i])
        for i, (src, dst) in enumerate(((a, a_out), (b, b_out), (c, c_out), (d, d_out), (e, e_out)))
    ]
    for copy in copies:
        copy.start()
    for copy in copies:
        copy.wait()


def fused(
    users, queries, key_rows, value_rows, gate_rows, item_emb, labels, propensity, requests, lengths, w_out
):
    _, rows, feats = queries.shape
    width = item_emb.shape[2]
    per_user = width // users
    nz = users // 4
    cols = feats // 2
    dma = pltpu.SemaphoreType.DMA
    block = (HEADS, rows, HEAD_DIM)
    square = (HEADS, rows, rows)
    vmem = pl.BlockSpec(memory_space=pltpu.VMEM)
    hbm = pl.BlockSpec(memory_space=pltpu.HBM)
    row = (1, rows)
    out = jax.ShapeDtypeStruct((rows, feats), F32)
    operands = [
        pltpu.with_memory_space_constraint(x, pltpu.HBM)
        for x in (
            queries[0], key_rows[0], value_rows[0], gate_rows[0], item_emb[0],
            labels, propensity, requests, w_out,
        )
    ]
    results = pl.pallas_call(
        functools.partial(fused_kernel, users),
        out_shape=[out, out, out, out, jax.ShapeDtypeStruct((per_user, cols), F32)],
        in_specs=[pl.BlockSpec(memory_space=pltpu.SMEM)] + [hbm] * 9,
        out_specs=[vmem] * 5,
        scratch_shapes=[pltpu.VMEM((rows, feats), BF16)] * 4
        + [
            pltpu.VMEM((rows, width), BF16),
            pltpu.VMEM(row, jnp.int32),
            pltpu.VMEM(row, F32),
            pltpu.VMEM(row, jnp.int32),
            pltpu.VMEM((feats, width // 2), BF16),
            dma((9,)),
            pltpu.VMEM(block, BF16),
            pltpu.VMEM(block, BF16),
            pltpu.VMEM(block, BF16),
            pltpu.VMEM(block, BF16),
            pltpu.VMEM((4, feats // 4, width // 2), BF16),
            pltpu.VMEM((8, rows), F32),
            pltpu.VMEM((8, rows), F32),
            pltpu.VMEM((HEADS - NEAR, rows, HEAD_DIM), BF16),
            pltpu.VMEM((HEADS - NEAR, rows, HEAD_DIM), BF16),
            pltpu.VMEM((2, rows, cols), BF16),
            pltpu.VMEM((users // 2, 2 * per_user, rows), BF16),
            pltpu.VMEM(square, BF16),
            pltpu.VMEM(square, F32),
            pltpu.VMEM(square, BF16),
            pltpu.VMEM(square, F32),
            pltpu.VMEM((rows, feats), F32),
            pltpu.VMEM((rows, feats), F32),
            pltpu.VMEM(block, BF16),
            pltpu.VMEM((2, 2, 2, nz, per_user, cols), BF16),
            pltpu.VMEM((2, 2, nz, per_user, cols), BF16),
            pltpu.VMEM((2, nz, per_user, cols), BF16),
            pltpu.VMEM((2, nz, per_user, cols), BF16),
            pltpu.VMEM((2, nz, per_user, cols), BF16),
            pltpu.VMEM((2, nz - 1, per_user, cols), BF16),
            pltpu.VMEM((per_user, cols), F32),
            pltpu.VMEM((per_user, cols), BF16),
            pltpu.VMEM((per_user, cols), BF16),
        ]
        + [dma((HEADS,))] * 8
        + [dma((5,))] * 2
        + [dma] * 2
        + [dma((HEADS - NEAR,))] * 2
        + [dma((2,))] * 4
        + [dma((2, nz - 1))] * 2
        + [dma] * 2,
        compiler_params=pltpu.CompilerParams(
            collective_id=0, has_side_effects=True, vmem_limit_bytes=48 * 1024 * 1024
        ),
        cost_estimate=pl.CostEstimate(
            flops=4 * 10**9, bytes_accessed=5 * 10**6, transcendentals=10**6
        ),
    )(lengths, *operands)
    dq, dk, dv, dgate, dw = pl.pallas_call(
        write_kernel,
        out_shape=[jax.ShapeDtypeStruct(r.shape, F32) for r in results],
        in_specs=[vmem] * 5,
        out_specs=[hbm] * 5,
        scratch_shapes=[dma((5,))],
        cost_estimate=pl.CostEstimate(flops=0, bytes_accessed=2 * 10**6, transcendentals=0),
    )(*results)
    return dq[None], dk[None], dv[None], dgate[None], dw.T


def solution(mesh):
    in_specs = (
        P("user", "ctx", None),
        P("user", "ctx", None),
        P("user", "ctx", None),
        P("user", "ctx", None),
        P("user", "ctx", None),
        P("user", "ctx"),
        P("user", "ctx"),
        P("user", "ctx"),
        P("user"),
        P(None, "ctx"),
    )
    out_specs = (
        P("user", "ctx", None),
        P("user", "ctx", None),
        P("user", "ctx", None),
        P("user", "ctx", None),
        P("ctx", "user"),
    )
    users = mesh.shape["user"]
    two_blocks = mesh.shape["ctx"] == 2 and users % 8 == 0
    step = functools.partial(fused, users) if two_blocks else local
    return jax.shard_map(step, mesh=mesh, in_specs=in_specs, out_specs=out_specs, check_vma=False)
```

```python
import functools
import math

import jax
import jax.numpy as jnp
from jax import lax
from jax.experimental import pallas as pl
from jax.experimental.pallas import tpu as pltpu
from jax.sharding import PartitionSpec as P

HEADS = 4
HEAD_DIM = 128
REQS = 64


norm_eps = 1e-06


def silu_slope(values):
    sigmoid_v = jax.nn.sigmoid(values)
    return sigmoid_v * (1.0 + values * (1.0 - sigmoid_v))


def split_heads(block):
    return block.reshape(block.shape[0], HEADS, HEAD_DIM)


def local(
    queries, key_rows, value_rows, gate_rows, item_emb, labels, propensity, requests, lengths, w_out
):
    row_count = queries.shape[1]
    feat_width = queries.shape[2]
    groups = lax.axis_size("ctx")
    seq_len = row_count * groups
    offset = lax.axis_index("ctx") * row_count
    score_factor = 1.0 / math.sqrt(HEAD_DIM)
    own_query = queries[0]
    own_key = key_rows[0]
    own_value = value_rows[0]
    query_h = split_heads(own_query)
    key_h = split_heads(own_key)
    value_h = split_heads(own_value)
    gate_f = gate_rows[0].astype(jnp.float32)
    hist_len = lengths[0]
    own_pos = offset + jnp.arange(row_count, dtype=jnp.int32)
    is_live = own_pos < hist_len
    key_piece = lax.all_gather(own_key, "ctx", axis=0, tiled=True)
    value_piece = lax.all_gather(own_value, "ctx", axis=0, tiled=True)
    piece_len = key_piece.shape[0]
    key_pos = jnp.arange(piece_len, dtype=jnp.int32)
    scores = (
        jnp.einsum(
            "qhd,khd->hqk", query_h, split_heads(key_piece), preferred_element_type=jnp.float32
        )
        * score_factor
    )
    allowed = (key_pos[None, :] <= own_pos[:, None]) & (key_pos[None, :] < hist_len)
    weights = (jnp.where(allowed[None], jax.nn.silu(scores), 0.0) / seq_len).astype(jnp.bfloat16)
    added = jnp.einsum(
        "hqk,khd->qhd", weights, split_heads(value_piece), preferred_element_type=jnp.float32
    )
    attended = added.reshape(row_count, feat_width)
    row_mean = jnp.mean(attended, axis=-1, keepdims=True)
    centered = attended - row_mean
    variance = jnp.mean(centered * centered, axis=-1, keepdims=True)
    inv_std = lax.rsqrt(variance + norm_eps)
    normed = centered * inv_std
    mixed_out = (normed * gate_f).astype(jnp.bfloat16)
    onehot = (requests[0][:, None] == jnp.arange(REQS, dtype=jnp.int32)[None, :]).astype(
        jnp.float32
    )
    live_f = is_live.astype(jnp.float32)
    inv_prop = jnp.where(is_live, 1.0 / propensity[0], 0.0)
    inv_sum, live_count = lax.psum(
        (jnp.sum(onehot * inv_prop[:, None], axis=0), jnp.sum(onehot * live_f[:, None], axis=0)),
        "ctx",
    )
    full_w = lax.all_gather(w_out, "ctx", axis=1, tiled=True)
    item_f = item_emb[0].astype(jnp.float32)
    item_proj = lax.dot_general(
        item_emb[0], full_w, (((1,), (1,)), ((), ())), preferred_element_type=jnp.float32
    )
    logits = jnp.sum(mixed_out.astype(jnp.float32) * item_proj, axis=-1)
    ratio = jnp.where(live_count > 0, live_count / jnp.where(live_count > 0, inv_sum, 1.0), 0.0)
    event_weight = inv_prop * jnp.sum(onehot * ratio[None, :], axis=-1)
    grad_logits = event_weight * (jax.nn.sigmoid(logits) - labels[0].astype(jnp.float32))
    grad_proj = (grad_logits[:, None] * item_f).astype(jnp.bfloat16)
    whole_grad = lax.dot_general(
        mixed_out, grad_proj, (((0,), (0,)), ((), ())), preferred_element_type=jnp.float32
    )
    partial_grad = lax.psum_scatter(whole_grad, "user", scatter_dimension=1, tiled=True)
    grad_w = lax.psum_scatter(partial_grad, "ctx", scatter_dimension=0, tiled=True)
    grad_mixed = grad_logits[:, None] * item_proj
    grad_gate = grad_mixed * normed
    grad_normed = grad_mixed * gate_f
    grad_attn = (
        grad_normed
        - jnp.mean(grad_normed, axis=-1, keepdims=True)
        - normed * jnp.mean(grad_normed * normed, axis=-1, keepdims=True)
    ) * inv_std
    grad_attn = grad_attn.astype(jnp.bfloat16)
    grad_attn_h = split_heads(grad_attn)
    key_piece = lax.all_gather(own_key, "ctx", axis=0, tiled=True)
    value_piece = lax.all_gather(own_value, "ctx", axis=0, tiled=True)
    piece_len = key_piece.shape[0]
    key_pos = jnp.arange(piece_len, dtype=jnp.int32)
    key_piece_h = split_heads(key_piece)
    scores = (
        jnp.einsum("qhd,khd->hqk", query_h, key_piece_h, preferred_element_type=jnp.float32)
        * score_factor
    )
    allowed = (key_pos[None, :] <= own_pos[:, None]) & (key_pos[None, :] < hist_len)
    grad_weights = jnp.einsum(
        "qhd,khd->hqk", grad_attn_h, split_heads(value_piece), preferred_element_type=jnp.float32
    )
    grad_scores = (
        jnp.where(allowed[None], grad_weights * silu_slope(scores), 0.0) / seq_len
    ).astype(jnp.bfloat16)
    added = (
        jnp.einsum("hqk,khd->qhd", grad_scores, key_piece_h, preferred_element_type=jnp.float32)
        * score_factor
    )
    grad_query = added.reshape(row_count, feat_width)
    query_piece = lax.all_gather(own_query, "ctx", axis=0, tiled=True)
    grad_piece = lax.all_gather(grad_attn, "ctx", axis=0, tiled=True)
    piece_len = query_piece.shape[0]
    query_pos = jnp.arange(piece_len, dtype=jnp.int32)
    query_piece_h = split_heads(query_piece)
    grad_piece_h = split_heads(grad_piece)
    scores = (
        jnp.einsum("qhd,khd->hqk", query_piece_h, key_h, preferred_element_type=jnp.float32)
        * score_factor
    )
    allowed = (own_pos[None, :] <= query_pos[:, None]) & (own_pos[None, :] < hist_len)
    weights = (jnp.where(allowed[None], jax.nn.silu(scores), 0.0) / seq_len).astype(jnp.bfloat16)
    grad_weights = jnp.einsum(
        "qhd,khd->hqk", grad_piece_h, value_h, preferred_element_type=jnp.float32
    )
    grad_scores = (
        jnp.where(allowed[None], grad_weights * silu_slope(scores), 0.0) / seq_len
    ).astype(jnp.bfloat16)
    added_key = (
        jnp.einsum("hqk,qhd->khd", grad_scores, query_piece_h, preferred_element_type=jnp.float32)
        * score_factor
    )
    added_value = jnp.einsum(
        "hqk,qhd->khd", weights, grad_piece_h, preferred_element_type=jnp.float32
    )
    grad_key = added_key.reshape(row_count, feat_width)
    grad_value = added_value.reshape(row_count, feat_width)
    return (grad_query[None], grad_key[None], grad_value[None], grad_gate[None], grad_w)


MESH = pl.DeviceIdType.MESH
F32 = jnp.float32
BF16 = jnp.bfloat16
NEAR = 2
W_FIRST = 1
PIECES = 4


def dot_nn(a, b):
    return lax.dot_general(a, b, (((1,), (0,)), ((), ())), preferred_element_type=F32)


def dot_nt(a, b):
    return lax.dot_general(a, b, (((1,), (1,)), ((), ())), preferred_element_type=F32)


def dot_tn(a, b):
    return lax.dot_general(a, b, (((0,), (0,)), ((), ())), preferred_element_type=F32)


def sigmoid(values):
    return 0.5 * jnp.tanh(0.5 * values) + 0.5


def head(h):
    return slice(h * HEAD_DIM, (h + 1) * HEAD_DIM)


def fused_kernel(
    users,
    len_ref, q_hbm, k_hbm, v_hbm, gate_hbm, item_hbm, lab_hbm, prop_hbm, req_hbm, w_hbm,
    dq_ref, dk_ref, dv_ref, dgate_ref, dw_ref,
    q_ref, k_ref, v_ref, gate_ref, item_ref, lab_ref, prop_ref, req_ref, w_ref, load,
    ok, ov, oq, oda, wbuf, stat_out, stat_in, part_out, part_in, mixed, item_t,
    wt, sl, wt_x, sl_x, att, u, da, gw,
    r_core, s_y, r_y, s_z, r_z, fin, s_x, r_x,
    ks, kr, vs, vr, qs, qr, das, dar, wss, wsr, sts, str_, ps, pr, cs, cr, ys, yr, zs, zr, xs, xr,
):
    rows, feats = q_ref.shape
    pairs = (
        (q_hbm, q_ref), (k_hbm, k_ref), (v_hbm, v_ref), (w_hbm, w_ref), (item_hbm, item_ref),
        (gate_hbm, gate_ref), (prop_hbm, prop_ref), (req_hbm, req_ref), (lab_hbm, lab_ref),
    )
    loads = [pltpu.make_async_copy(a, b, load.at[i]) for i, (a, b) in enumerate(pairs)]
    for copy in loads:
        copy.start()
    width = item_ref.shape[1]
    half_w = width // 2
    seq_len = 2 * rows
    nz = users // 4
    cols = feats // 2
    factor = 1.0 / math.sqrt(HEAD_DIM)
    ctx = lax.axis_index("ctx")
    user = lax.axis_index("user")
    core = lax.rem(user, 2)
    yy = lax.rem(lax.div(user, 2), 2)
    zz = lax.div(user, 4)
    quarter = lax.rem(user, 4)
    offset = ctx * rows
    x_peer = (1 - ctx, user)
    c_peer = (ctx, user + 1 - 2 * core)
    y_peer = (ctx, user + 2 - 4 * yy)
    pair_peer = (ctx, quarter + 4 * (zz + 1 - 2 * lax.rem(zz, 2)))
    z_peers = [(ctx, quarter + 4 * lax.rem(zz + step, nz)) for step in range(1, nz)]

    def remote(source, target, send_sem, recv_sem, device):
        return pltpu.make_async_remote_copy(
            src_ref=source, dst_ref=target, send_sem=send_sem, recv_sem=recv_sem,
            device_id=device, device_id_type=MESH,
        )

    peers = [x_peer, c_peer, y_peer] + z_peers
    barrier = pltpu.get_barrier_semaphore()
    for peer in peers:
        pl.semaphore_signal(barrier, inc=1, device_id=peer, device_id_type=MESH)
    pl.semaphore_wait(barrier, len(peers))

    stat_copy = remote(stat_out, stat_in, sts, str_, x_peer)
    w_part = feats // 4
    w_slice = w_part // 2
    w_at = pl.multiple_of(lax.rem(zz, 2) * w_slice, w_slice)
    w_next = pl.multiple_of((1 - lax.rem(zz, 2)) * w_slice, w_slice)
    w_rows = pl.ds(pl.multiple_of(quarter * w_part, w_part) + w_at, w_slice)
    far = quarter + 2 - 4 * yy

    def spread(i, quarter_at, row_at, peer):
        rows_at = wbuf.at[quarter_at, pl.ds(row_at, w_slice)]
        return remote(rows_at, rows_at, wss.at[i], wsr.at[i], peer)

    w_copy = remote(w_hbm.at[w_rows], wbuf.at[quarter, pl.ds(w_at, w_slice)], wss.at[0], wsr.at[0], x_peer)
    w_pair = spread(1, quarter, w_at, pair_peer)
    w_y = [spread(2, quarter, w_at, y_peer), spread(3, quarter, w_next, y_peer)]
    w_core = [spread(4, quarter, w_at, c_peer), spread(5, quarter, w_next, c_peer)]
    w_far = [spread(6, far, w_at, c_peer), spread(7, far, w_next, c_peer)]
    w_all = [w_copy, w_pair] + w_y + w_core + w_far
    k_copy = [remote(k_hbm.at[:, head(h)], ok.at[h], ks.at[h], kr.at[h], x_peer) for h in range(HEADS)]
    v_copy = [remote(v_hbm.at[:, head(h)], ov.at[h], vs.at[h], vr.at[h], x_peer) for h in range(HEADS)]
    q_copy = [remote(q_hbm.at[:, head(h)], oq.at[h], qs.at[h], qr.at[h], x_peer) for h in range(HEADS)]
    da_copy = [remote(da.at[h], oda.at[h], das.at[h], dar.at[h], x_peer) for h in range(HEADS)]

    part_copy = [remote(part_out.at[i], part_in.at[i], ps.at[i], pr.at[i], x_peer) for i in range(HEADS - NEAR)]
    w_copy.start()

    @pl.when(ctx == 0)
    def _():
        for h in range(NEAR):
            k_copy[h].start()
            v_copy[h].start()

    @pl.when(ctx == 1)
    def _():
        for h in range(NEAR, HEADS):
            q_copy[h].start()
        for h in range(NEAR):
            q_copy[h].start()

    for copy in loads:
        copy.wait()
    hist_len = len_ref[0]
    reqs = req_ref[...]
    onehot = (lax.broadcasted_iota(jnp.int32, (REQS, rows), 0) == reqs).astype(F32)
    live = offset + lax.broadcasted_iota(jnp.int32, (1, rows), 1) < hist_len
    inv_prop = jnp.where(live, 1.0 / prop_ref[...], 0.0)
    live_f = jnp.where(live, 1.0, 0.0)
    stat_out[0:1] = reqs.astype(F32)
    stat_out[1:2] = inv_prop
    stat_out[2:3] = live_f
    stat_out[3:8] = jnp.zeros((5, rows), F32)

    stat_copy.start()

    def gates(scores, allowed):
        s = scores * factor
        sig = sigmoid(s)
        weight = jnp.where(allowed, s * sig, 0.0) * (1.0 / seq_len)
        slope = jnp.where(allowed, sig * (1.0 + s * (1.0 - sig)), 0.0) * (1.0 / seq_len)
        return weight.astype(BF16), slope

    row_i = lax.broadcasted_iota(jnp.int32, (rows, rows), 0)
    col_i = lax.broadcasted_iota(jnp.int32, (rows, rows), 1)
    allowed = (col_i <= row_i) & (offset + col_i < hist_len)
    for h in range(HEADS):
        weight, slope = gates(dot_nt(q_ref[:, head(h)], k_ref[:, head(h)]), allowed)
        wt[h] = weight
        sl[h] = slope
        att[:, head(h)] = dot_nn(weight, v_ref[:, head(h)])
        if h == W_FIRST:
            w_copy.wait_recv()
            w_pair.start()
            w_y[0].start()
            w_core[0].start()

    w_pair.wait_recv()
    w_y[1].start()
    w_core[1].start()

    own_cols = pl.ds(pl.multiple_of(ctx * half_w, half_w), half_w)
    other_cols = pl.ds(pl.multiple_of((1 - ctx) * half_w, half_w), half_w)
    seen = lax.broadcasted_iota(jnp.int32, (rows, rows), 1) < hist_len

    def cross_scores(h):
        q_copy[h].wait_recv()
        weight, slope = gates(dot_nt(oq[h], k_ref[:, head(h)]), seen)
        wt_x[h] = weight
        sl_x[h] = slope

    @pl.when(ctx == 0)
    def _():
        for h in range(NEAR, HEADS):
            cross_scores(h)
            part_out[h - NEAR] = dot_nn(wt_x[h], v_ref[:, head(h)]).astype(BF16)
            part_copy[h - NEAR].start()
        for h in range(NEAR, HEADS):
            k_copy[h].start()
            v_copy[h].start()

    u[...] = dot_nt(item_ref[:, own_cols], w_ref[...])
    per_user = width // users
    for j in range(users // 2):
        item_t[j] = item_ref[:, j * 2 * per_user : (j + 1) * 2 * per_user].T

    w_y[0].wait_recv()
    w_far[0].start()

    def look_back(h):
        k_copy[h].wait_recv()
        weight, slope = gates(dot_nt(q_ref[:, head(h)], ok[h]), seen)
        sl_x[h] = slope
        v_copy[h].wait_recv()
        att[:, head(h)] += dot_nn(weight, ov[h])

    @pl.when(ctx == 1)
    def _():
        look_back(0)

    w_y[1].wait_recv()
    w_far[1].start()

    @pl.when(ctx == 1)
    def _():
        for h in range(1, NEAR):
            look_back(h)
        for h in range(NEAR, HEADS):
            part_copy[h - NEAR].wait_recv()
            att[:, head(h)] += part_in[h - NEAR].astype(F32)

    for copy in w_core + w_far:
        copy.wait_recv()
    for part in range(4):
        part_cols = slice(part * w_part, (part + 1) * w_part)
        u[:, part_cols] += dot_nt(item_ref[:, other_cols], wbuf[part])

    attended = att[...]
    centered = attended - jnp.mean(attended, axis=-1, keepdims=True)
    inv_std = lax.rsqrt(jnp.mean(centered * centered, axis=-1, keepdims=True) + norm_eps)
    normed = centered * inv_std
    gate_f = gate_ref[...].astype(F32)
    mixed_out = (normed * gate_f).astype(BF16)
    item_proj = u[...]
    logits = jnp.sum(mixed_out.astype(F32) * item_proj, axis=-1, keepdims=True)

    stat_copy.wait_recv()
    onehot_x = (
        lax.broadcasted_iota(jnp.int32, (REQS, rows), 0) == stat_in[0:1].astype(jnp.int32)
    ).astype(F32)
    inv_sum = jnp.sum(onehot * inv_prop + onehot_x * stat_in[1:2], axis=1, keepdims=True)
    live_count = jnp.sum(onehot * live_f + onehot_x * stat_in[2:3], axis=1, keepdims=True)
    some = live_count > 0
    ratio = jnp.where(some, live_count / jnp.where(some, inv_sum, 1.0), 0.0)
    event_weight = inv_prop * jnp.sum(onehot * ratio, axis=0, keepdims=True)
    eye = row_i == col_i
    weight_col = jnp.sum(jnp.where(eye, event_weight, 0.0), axis=1, keepdims=True)
    label_col = jnp.sum(jnp.where(eye, lab_ref[...].astype(F32), 0.0), axis=1, keepdims=True)
    grad_logits = weight_col * (jax.nn.sigmoid(logits) - label_col)
    weighted = (grad_logits * mixed_out.astype(F32)).astype(BF16)
    for half in range(2):
        mixed[half] = weighted[:, half * cols : (half + 1) * cols]
    halves = [1 - ctx, ctx]
    piece = feats // PIECES
    c_copy = [remote(gw.at[1 - core, o], r_core.at[o], cs.at[o], cr.at[o], c_peer) for o in range(PIECES)]
    y_copy = [remote(s_y.at[o], r_y.at[o], ys.at[o], yr.at[o], y_peer) for o in range(PIECES)]
    z_copy = [
        [
            remote(
                s_z.at[o, lax.rem(zz + i + 1, nz)], r_z.at[o, i], zs.at[o, i], zr.at[o, i], z_peers[i]
            )
            for i in range(nz - 1)
        ]
        for o in range(PIECES)
    ]
    x_copy = [remote(s_x.at[o], r_x.at[o], xs.at[o], xr.at[o], x_peer) for o in range(PIECES // 2)]
    def weight_grad(o):
        for j in range(users // 2):
            chunk = dot_nn(item_t[j], mixed[halves[o]]).astype(BF16)
            for c in range(2):
                for p in range(PIECES // 2):
                    gw[c, o * PIECES // 2 + p, j % 2, j // 2] = chunk[
                        c * per_user : (c + 1) * per_user, p * piece : (p + 1) * piece
                    ]
        for p in range(PIECES // 2):
            c_copy[o * PIECES // 2 + p].start()

    weight_grad(0)
    weight_grad(1)
    grad_mixed = grad_logits * item_proj
    dgate_ref[...] = grad_mixed * normed
    grad_normed = grad_mixed * gate_f
    grad_attn = (
        grad_normed
        - jnp.mean(grad_normed, axis=-1, keepdims=True)
        - normed * jnp.mean(grad_normed * normed, axis=-1, keepdims=True)
    ) * inv_std
    for h in range(HEADS):
        da[h] = grad_attn[:, head(h)].astype(BF16)

    @pl.when(ctx == 1)
    def _():
        for h in range(HEADS):
            da_copy[h].start()

    def after_core(o):
        c_copy[o].wait_recv()
        s_y[o] = (gw[core, o, 1 - yy].astype(F32) + r_core[o, 1 - yy].astype(F32)).astype(BF16)
        y_copy[o].start()

    def after_y(o):
        y_copy[o].wait_recv()
        mine = gw[core, o, yy].astype(F32) + r_core[o, yy].astype(F32)
        s_z[o] = (mine + r_y[o].astype(F32)).astype(BF16)
        for copy in z_copy[o]:
            copy.start()

    def after_z(o):
        total = gw[core, o, yy, zz].astype(F32) + r_core[o, yy, zz].astype(F32)
        total += r_y[o, zz].astype(F32)
        for i in range(nz - 1):
            z_copy[o][i].wait_recv()
            total += r_z[o, i].astype(F32)
        if o < PIECES // 2:
            s_x[o] = total.astype(BF16)
            x_copy[o].start()
        else:
            fin[o - PIECES // 2] = total

    def backward(h):
        grad_scores = (dot_nt(da[h], v_ref[:, head(h)]) * sl[h]).astype(BF16)
        dq_ref[:, head(h)] = dot_nn(grad_scores, k_ref[:, head(h)]) * factor
        dk_ref[:, head(h)] = dot_tn(grad_scores, q_ref[:, head(h)]) * factor
        dv_ref[:, head(h)] = dot_tn(wt[h], da[h])

    def cross_query(h):
        grad_scores = (dot_nt(da[h], ov[h]) * sl_x[h]).astype(BF16)
        dq_ref[:, head(h)] += dot_nn(grad_scores, ok[h]) * factor

    def cross_key(h):
        da_copy[h].wait_recv()
        grad_scores = (dot_nt(oda[h], v_ref[:, head(h)]) * sl_x[h]).astype(BF16)
        dk_ref[:, head(h)] += dot_tn(grad_scores, oq[h]) * factor
        dv_ref[:, head(h)] += dot_tn(wt_x[h], oda[h])

    for o in range(PIECES):
        after_core(o)
    for h in range(HEADS):
        backward(h)
        if h > 0:
            after_y(h - 1)

    @pl.when(ctx == 0)
    def _():
        for h in range(NEAR):
            cross_scores(h)

    @pl.when(ctx == 1)
    def _():
        for h in range(NEAR):
            cross_query(h)

    after_y(3)

    @pl.when(ctx == 1)
    def _():
        for h in range(NEAR, HEADS):
            k_copy[h].wait_recv()
            v_copy[h].wait_recv()
            sl_x[h] = gates(dot_nt(q_ref[:, head(h)], ok[h]), seen)[1]
            cross_query(h)

    for o in range(PIECES):
        after_z(o)

    @pl.when(ctx == 0)
    def _():
        for h in range(HEADS):
            cross_key(h)
        for h in range(HEADS):
            k_copy[h].wait_send()
            v_copy[h].wait_send()
        for copy in part_copy:
            copy.wait_send()

    @pl.when(ctx == 1)
    def _():
        for h in range(HEADS):
            q_copy[h].wait_send()
            da_copy[h].wait_send()

    for o in range(PIECES // 2):
        x_copy[o].wait_recv()
        dw_ref[:, o * piece : (o + 1) * piece] = fin[o] + r_x[o].astype(F32)
    for copy in [stat_copy] + x_copy + w_all + c_copy + y_copy + sum(z_copy, []):
        copy.wait_send()


def write_kernel(a, b, c, d, e, a_out, b_out, c_out, d_out, e_out, sems):
    copies = [
        pltpu.make_async_copy(src, dst, sems.at[i])
        for i, (src, dst) in enumerate(((a, a_out), (b, b_out), (c, c_out), (d, d_out), (e, e_out)))
    ]
    for copy in copies:
        copy.start()
    for copy in copies:
        copy.wait()


def fused(
    users, queries, key_rows, value_rows, gate_rows, item_emb, labels, propensity, requests, lengths, w_out
):
    _, rows, feats = queries.shape
    width = item_emb.shape[2]
    per_user = width // users
    nz = users // 4
    cols = feats // 2
    piece = feats // PIECES
    dma = pltpu.SemaphoreType.DMA
    block = (HEADS, rows, HEAD_DIM)
    square = (HEADS, rows, rows)
    vmem = pl.BlockSpec(memory_space=pltpu.VMEM)
    hbm = pl.BlockSpec(memory_space=pltpu.HBM)
    row = (1, rows)
    out = jax.ShapeDtypeStruct((rows, feats), F32)
    operands = [
        pltpu.with_memory_space_constraint(x, pltpu.HBM)
        for x in (
            queries[0], key_rows[0], value_rows[0], gate_rows[0], item_emb[0],
            labels, propensity, requests, w_out,
        )
    ]
    results = pl.pallas_call(
        functools.partial(fused_kernel, users),
        out_shape=[out, out, out, out, jax.ShapeDtypeStruct((per_user, cols), F32)],
        in_specs=[pl.BlockSpec(memory_space=pltpu.SMEM)] + [hbm] * 9,
        out_specs=[vmem] * 5,
        scratch_shapes=[pltpu.VMEM((rows, feats), BF16)] * 4
        + [
            pltpu.VMEM((rows, width), BF16),
            pltpu.VMEM(row, jnp.int32),
            pltpu.VMEM(row, F32),
            pltpu.VMEM(row, jnp.int32),
            pltpu.VMEM((feats, width // 2), BF16),
            dma((9,)),
            pltpu.VMEM(block, BF16),
            pltpu.VMEM(block, BF16),
            pltpu.VMEM(block, BF16),
            pltpu.VMEM(block, BF16),
            pltpu.VMEM((4, feats // 4, width // 2), BF16),
            pltpu.VMEM((8, rows), F32),
            pltpu.VMEM((8, rows), F32),
            pltpu.VMEM((HEADS - NEAR, rows, HEAD_DIM), BF16),
            pltpu.VMEM((HEADS - NEAR, rows, HEAD_DIM), BF16),
            pltpu.VMEM((2, rows, cols), BF16),
            pltpu.VMEM((users // 2, 2 * per_user, rows), BF16),
            pltpu.VMEM(square, BF16),
            pltpu.VMEM(square, F32),
            pltpu.VMEM(square, BF16),
            pltpu.VMEM(square, F32),
            pltpu.VMEM((rows, feats), F32),
            pltpu.VMEM((rows, feats), F32),
            pltpu.VMEM(block, BF16),
            pltpu.VMEM((2, PIECES, 2, nz, per_user, piece), BF16),
            pltpu.VMEM((PIECES, 2, nz, per_user, piece), BF16),
            pltpu.VMEM((PIECES, nz, per_user, piece), BF16),
            pltpu.VMEM((PIECES, nz, per_user, piece), BF16),
            pltpu.VMEM((PIECES, nz, per_user, piece), BF16),
            pltpu.VMEM((PIECES, nz - 1, per_user, piece), BF16),
            pltpu.VMEM((PIECES // 2, per_user, piece), F32),
            pltpu.VMEM((PIECES // 2, per_user, piece), BF16),
            pltpu.VMEM((PIECES // 2, per_user, piece), BF16),
        ]
        + [dma((HEADS,))] * 8
        + [dma((8,))] * 2
        + [dma] * 2
        + [dma((HEADS - NEAR,))] * 2
        + [dma((PIECES,))] * 4
        + [dma((PIECES, nz - 1))] * 2
        + [dma((PIECES // 2,))] * 2,
        compiler_params=pltpu.CompilerParams(
            collective_id=0, has_side_effects=True, vmem_limit_bytes=48 * 1024 * 1024
        ),
        cost_estimate=pl.CostEstimate(
            flops=4 * 10**9, bytes_accessed=5 * 10**6, transcendentals=10**6
        ),
    )(lengths, *operands)
    dq, dk, dv, dgate, dw = pl.pallas_call(
        write_kernel,
        out_shape=[jax.ShapeDtypeStruct(r.shape, F32) for r in results],
        in_specs=[vmem] * 5,
        out_specs=[hbm] * 5,
        scratch_shapes=[dma((5,))],
        compiler_params=pltpu.CompilerParams(vmem_limit_bytes=4 * 1024 * 1024),
        cost_estimate=pl.CostEstimate(flops=0, bytes_accessed=2 * 10**6, transcendentals=0),
    )(*[pltpu.with_memory_space_constraint(r, pltpu.VMEM) for r in results])
    return dq[None], dk[None], dv[None], dgate[None], dw.T


def solution(mesh):
    in_specs = (
        P("user", "ctx", None),
        P("user", "ctx", None),
        P("user", "ctx", None),
        P("user", "ctx", None),
        P("user", "ctx", None),
        P("user", "ctx"),
        P("user", "ctx"),
        P("user", "ctx"),
        P("user"),
        P(None, "ctx"),
    )
    out_specs = (
        P("user", "ctx", None),
        P("user", "ctx", None),
        P("user", "ctx", None),
        P("user", "ctx", None),
        P("ctx", "user"),
    )
    users = mesh.shape["user"]
    two_blocks = mesh.shape["ctx"] == 2 and users % 8 == 0
    step = functools.partial(fused, users) if two_blocks else local
    return jax.shard_map(step, mesh=mesh, in_specs=in_specs, out_specs=out_specs, check_vma=False)
```

```python
import functools
import math

import jax
import jax.numpy as jnp
from jax import lax
from jax.experimental import pallas as pl
from jax.experimental.pallas import tpu as pltpu
from jax.sharding import PartitionSpec as P

HEADS = 4
HEAD_DIM = 128
REQS = 64


norm_eps = 1e-06


def silu_slope(values):
    sigmoid_v = jax.nn.sigmoid(values)
    return sigmoid_v * (1.0 + values * (1.0 - sigmoid_v))


def split_heads(block):
    return block.reshape(block.shape[0], HEADS, HEAD_DIM)


def local(
    queries, key_rows, value_rows, gate_rows, item_emb, labels, propensity, requests, lengths, w_out
):
    row_count = queries.shape[1]
    feat_width = queries.shape[2]
    groups = lax.axis_size("ctx")
    seq_len = row_count * groups
    offset = lax.axis_index("ctx") * row_count
    score_factor = 1.0 / math.sqrt(HEAD_DIM)
    own_query = queries[0]
    own_key = key_rows[0]
    own_value = value_rows[0]
    query_h = split_heads(own_query)
    key_h = split_heads(own_key)
    value_h = split_heads(own_value)
    gate_f = gate_rows[0].astype(jnp.float32)
    hist_len = lengths[0]
    own_pos = offset + jnp.arange(row_count, dtype=jnp.int32)
    is_live = own_pos < hist_len
    key_piece = lax.all_gather(own_key, "ctx", axis=0, tiled=True)
    value_piece = lax.all_gather(own_value, "ctx", axis=0, tiled=True)
    piece_len = key_piece.shape[0]
    key_pos = jnp.arange(piece_len, dtype=jnp.int32)
    scores = (
        jnp.einsum(
            "qhd,khd->hqk", query_h, split_heads(key_piece), preferred_element_type=jnp.float32
        )
        * score_factor
    )
    allowed = (key_pos[None, :] <= own_pos[:, None]) & (key_pos[None, :] < hist_len)
    weights = (jnp.where(allowed[None], jax.nn.silu(scores), 0.0) / seq_len).astype(jnp.bfloat16)
    added = jnp.einsum(
        "hqk,khd->qhd", weights, split_heads(value_piece), preferred_element_type=jnp.float32
    )
    attended = added.reshape(row_count, feat_width)
    row_mean = jnp.mean(attended, axis=-1, keepdims=True)
    centered = attended - row_mean
    variance = jnp.mean(centered * centered, axis=-1, keepdims=True)
    inv_std = lax.rsqrt(variance + norm_eps)
    normed = centered * inv_std
    mixed_out = (normed * gate_f).astype(jnp.bfloat16)
    onehot = (requests[0][:, None] == jnp.arange(REQS, dtype=jnp.int32)[None, :]).astype(
        jnp.float32
    )
    live_f = is_live.astype(jnp.float32)
    inv_prop = jnp.where(is_live, 1.0 / propensity[0], 0.0)
    inv_sum, live_count = lax.psum(
        (jnp.sum(onehot * inv_prop[:, None], axis=0), jnp.sum(onehot * live_f[:, None], axis=0)),
        "ctx",
    )
    full_w = lax.all_gather(w_out, "ctx", axis=1, tiled=True)
    item_f = item_emb[0].astype(jnp.float32)
    item_proj = lax.dot_general(
        item_emb[0], full_w, (((1,), (1,)), ((), ())), preferred_element_type=jnp.float32
    )
    logits = jnp.sum(mixed_out.astype(jnp.float32) * item_proj, axis=-1)
    ratio = jnp.where(live_count > 0, live_count / jnp.where(live_count > 0, inv_sum, 1.0), 0.0)
    event_weight = inv_prop * jnp.sum(onehot * ratio[None, :], axis=-1)
    grad_logits = event_weight * (jax.nn.sigmoid(logits) - labels[0].astype(jnp.float32))
    grad_proj = (grad_logits[:, None] * item_f).astype(jnp.bfloat16)
    whole_grad = lax.dot_general(
        mixed_out, grad_proj, (((0,), (0,)), ((), ())), preferred_element_type=jnp.float32
    )
    partial_grad = lax.psum_scatter(whole_grad, "user", scatter_dimension=1, tiled=True)
    grad_w = lax.psum_scatter(partial_grad, "ctx", scatter_dimension=0, tiled=True)
    grad_mixed = grad_logits[:, None] * item_proj
    grad_gate = grad_mixed * normed
    grad_normed = grad_mixed * gate_f
    grad_attn = (
        grad_normed
        - jnp.mean(grad_normed, axis=-1, keepdims=True)
        - normed * jnp.mean(grad_normed * normed, axis=-1, keepdims=True)
    ) * inv_std
    grad_attn = grad_attn.astype(jnp.bfloat16)
    grad_attn_h = split_heads(grad_attn)
    key_piece = lax.all_gather(own_key, "ctx", axis=0, tiled=True)
    value_piece = lax.all_gather(own_value, "ctx", axis=0, tiled=True)
    piece_len = key_piece.shape[0]
    key_pos = jnp.arange(piece_len, dtype=jnp.int32)
    key_piece_h = split_heads(key_piece)
    scores = (
        jnp.einsum("qhd,khd->hqk", query_h, key_piece_h, preferred_element_type=jnp.float32)
        * score_factor
    )
    allowed = (key_pos[None, :] <= own_pos[:, None]) & (key_pos[None, :] < hist_len)
    grad_weights = jnp.einsum(
        "qhd,khd->hqk", grad_attn_h, split_heads(value_piece), preferred_element_type=jnp.float32
    )
    grad_scores = (
        jnp.where(allowed[None], grad_weights * silu_slope(scores), 0.0) / seq_len
    ).astype(jnp.bfloat16)
    added = (
        jnp.einsum("hqk,khd->qhd", grad_scores, key_piece_h, preferred_element_type=jnp.float32)
        * score_factor
    )
    grad_query = added.reshape(row_count, feat_width)
    query_piece = lax.all_gather(own_query, "ctx", axis=0, tiled=True)
    grad_piece = lax.all_gather(grad_attn, "ctx", axis=0, tiled=True)
    piece_len = query_piece.shape[0]
    query_pos = jnp.arange(piece_len, dtype=jnp.int32)
    query_piece_h = split_heads(query_piece)
    grad_piece_h = split_heads(grad_piece)
    scores = (
        jnp.einsum("qhd,khd->hqk", query_piece_h, key_h, preferred_element_type=jnp.float32)
        * score_factor
    )
    allowed = (own_pos[None, :] <= query_pos[:, None]) & (own_pos[None, :] < hist_len)
    weights = (jnp.where(allowed[None], jax.nn.silu(scores), 0.0) / seq_len).astype(jnp.bfloat16)
    grad_weights = jnp.einsum(
        "qhd,khd->hqk", grad_piece_h, value_h, preferred_element_type=jnp.float32
    )
    grad_scores = (
        jnp.where(allowed[None], grad_weights * silu_slope(scores), 0.0) / seq_len
    ).astype(jnp.bfloat16)
    added_key = (
        jnp.einsum("hqk,qhd->khd", grad_scores, query_piece_h, preferred_element_type=jnp.float32)
        * score_factor
    )
    added_value = jnp.einsum(
        "hqk,qhd->khd", weights, grad_piece_h, preferred_element_type=jnp.float32
    )
    grad_key = added_key.reshape(row_count, feat_width)
    grad_value = added_value.reshape(row_count, feat_width)
    return (grad_query[None], grad_key[None], grad_value[None], grad_gate[None], grad_w)


MESH = pl.DeviceIdType.MESH
F32 = jnp.float32
BF16 = jnp.bfloat16
NEAR = 2
W_FIRST = 1
PIECES = 4


def dot_nn(a, b):
    return lax.dot_general(a, b, (((1,), (0,)), ((), ())), preferred_element_type=F32)


def dot_nt(a, b):
    return lax.dot_general(a, b, (((1,), (1,)), ((), ())), preferred_element_type=F32)


def dot_tn(a, b):
    return lax.dot_general(a, b, (((0,), (0,)), ((), ())), preferred_element_type=F32)


def sigmoid(values):
    return 0.5 * jnp.tanh(0.5 * values) + 0.5


def head(h):
    return slice(h * HEAD_DIM, (h + 1) * HEAD_DIM)


def fused_kernel(
    users,
    len_ref, q_hbm, k_hbm, v_hbm, gate_hbm, item_hbm, lab_hbm, prop_hbm, req_hbm, w_hbm,
    dq_ref, dk_ref, dv_ref, dgate_ref, dw_ref,
    q_ref, k_ref, v_ref, gate_ref, item_ref, lab_ref, prop_ref, req_ref, w_ref, load,
    ok, ov, oq, oda, wbuf, stat_out, stat_in, part_out, part_in, mixed, item_t,
    wt, sl, wt_x, sl_x, att, u, da, gw,
    r_core, s_y, r_y, s_z, r_z, fin, s_x, r_x,
    ks, kr, vs, vr, qs, qr, das, dar, wss, wsr, sts, str_, ps, pr, cs, cr, ys, yr, zs, zr, xs, xr,
):
    rows, feats = q_ref.shape
    pairs = (
        (q_hbm, q_ref), (k_hbm, k_ref), (v_hbm, v_ref), (w_hbm, w_ref), (item_hbm, item_ref),
        (gate_hbm, gate_ref), (prop_hbm, prop_ref), (req_hbm, req_ref), (lab_hbm, lab_ref),
    )
    loads = [pltpu.make_async_copy(a, b, load.at[i]) for i, (a, b) in enumerate(pairs)]
    for copy in loads:
        copy.start()
    width = item_ref.shape[1]
    half_w = width // 2
    seq_len = 2 * rows
    nz = users // 4
    cols = feats // 2
    factor = 1.0 / math.sqrt(HEAD_DIM)
    ctx = lax.axis_index("ctx")
    user = lax.axis_index("user")
    core = lax.rem(user, 2)
    yy = lax.rem(lax.div(user, 2), 2)
    zz = lax.div(user, 4)
    quarter = lax.rem(user, 4)
    offset = ctx * rows
    x_peer = (1 - ctx, user)
    c_peer = (ctx, user + 1 - 2 * core)
    y_peer = (ctx, user + 2 - 4 * yy)
    pair_peer = (ctx, quarter + 4 * (zz + 1 - 2 * lax.rem(zz, 2)))
    z_peers = [(ctx, quarter + 4 * lax.rem(zz + step, nz)) for step in range(1, nz)]

    def remote(source, target, send_sem, recv_sem, device):
        return pltpu.make_async_remote_copy(
            src_ref=source, dst_ref=target, send_sem=send_sem, recv_sem=recv_sem,
            device_id=device, device_id_type=MESH,
        )

    peers = [x_peer, c_peer, y_peer] + z_peers
    barrier = pltpu.get_barrier_semaphore()
    for peer in peers:
        pl.semaphore_signal(barrier, inc=1, device_id=peer, device_id_type=MESH)
    pl.semaphore_wait(barrier, len(peers))

    stat_copy = remote(stat_out, stat_in, sts, str_, x_peer)
    w_part = feats // 4
    w_slice = w_part // 2
    w_at = pl.multiple_of(lax.rem(zz, 2) * w_slice, w_slice)
    w_next = pl.multiple_of((1 - lax.rem(zz, 2)) * w_slice, w_slice)
    w_rows = pl.ds(pl.multiple_of(quarter * w_part, w_part) + w_at, w_slice)
    far = quarter + 2 - 4 * yy

    def spread(i, quarter_at, row_at, peer):
        rows_at = wbuf.at[quarter_at, pl.ds(row_at, w_slice)]
        return remote(rows_at, rows_at, wss.at[i], wsr.at[i], peer)

    w_copy = remote(w_hbm.at[w_rows], wbuf.at[quarter, pl.ds(w_at, w_slice)], wss.at[0], wsr.at[0], x_peer)
    w_pair = spread(1, quarter, w_at, pair_peer)
    w_y = [spread(2, quarter, w_at, y_peer), spread(3, quarter, w_next, y_peer)]
    w_core = [spread(4, quarter, w_at, c_peer), spread(5, quarter, w_next, c_peer)]
    w_far = [spread(6, far, w_at, c_peer), spread(7, far, w_next, c_peer)]
    w_all = [w_copy, w_pair] + w_y + w_core + w_far
    k_copy = [remote(k_hbm.at[:, head(h)], ok.at[h], ks.at[h], kr.at[h], x_peer) for h in range(HEADS)]
    v_copy = [remote(v_hbm.at[:, head(h)], ov.at[h], vs.at[h], vr.at[h], x_peer) for h in range(HEADS)]
    q_copy = [remote(q_hbm.at[:, head(h)], oq.at[h], qs.at[h], qr.at[h], x_peer) for h in range(HEADS)]
    da_copy = [remote(da.at[h], oda.at[h], das.at[h], dar.at[h], x_peer) for h in range(HEADS)]

    part_copy = [remote(part_out.at[i], part_in.at[i], ps.at[i], pr.at[i], x_peer) for i in range(HEADS - NEAR)]
    w_copy.start()

    @pl.when(ctx == 0)
    def _():
        for h in range(NEAR):
            k_copy[h].start()
            v_copy[h].start()

    @pl.when(ctx == 1)
    def _():
        for h in range(NEAR, HEADS):
            q_copy[h].start()
        for h in range(NEAR):
            q_copy[h].start()

    for copy in loads:
        copy.wait()
    hist_len = len_ref[0]
    reqs = req_ref[...]
    onehot = (lax.broadcasted_iota(jnp.int32, (REQS, rows), 0) == reqs).astype(F32)
    live = offset + lax.broadcasted_iota(jnp.int32, (1, rows), 1) < hist_len
    inv_prop = jnp.where(live, 1.0 / prop_ref[...], 0.0)
    live_f = jnp.where(live, 1.0, 0.0)
    stat_out[0:1] = reqs.astype(F32)
    stat_out[1:2] = inv_prop
    stat_out[2:3] = live_f
    stat_out[3:8] = jnp.zeros((5, rows), F32)

    stat_copy.start()

    def gates(scores, allowed):
        s = scores * factor
        sig = sigmoid(s)
        weight = jnp.where(allowed, s * sig, 0.0) * (1.0 / seq_len)
        slope = jnp.where(allowed, sig * (1.0 + s * (1.0 - sig)), 0.0) * (1.0 / seq_len)
        return weight.astype(BF16), slope

    row_i = lax.broadcasted_iota(jnp.int32, (rows, rows), 0)
    col_i = lax.broadcasted_iota(jnp.int32, (rows, rows), 1)
    allowed = (col_i <= row_i) & (offset + col_i < hist_len)
    for h in range(HEADS):
        weight, slope = gates(dot_nt(q_ref[:, head(h)], k_ref[:, head(h)]), allowed)
        wt[h] = weight
        sl[h] = slope
        att[:, head(h)] = dot_nn(weight, v_ref[:, head(h)])
        if h == W_FIRST:
            w_copy.wait_recv()
            w_pair.start()
            w_y[0].start()
            w_core[0].start()

    w_pair.wait_recv()
    w_y[1].start()
    w_core[1].start()

    own_cols = pl.ds(pl.multiple_of(ctx * half_w, half_w), half_w)
    other_cols = pl.ds(pl.multiple_of((1 - ctx) * half_w, half_w), half_w)
    seen = lax.broadcasted_iota(jnp.int32, (rows, rows), 1) < hist_len

    def cross_scores(h):
        q_copy[h].wait_recv()
        weight, slope = gates(dot_nt(oq[h], k_ref[:, head(h)]), seen)
        wt_x[h] = weight
        sl_x[h] = slope

    @pl.when(ctx == 0)
    def _():
        for h in range(NEAR, HEADS):
            cross_scores(h)
            part_out[h - NEAR] = dot_nn(wt_x[h], v_ref[:, head(h)]).astype(BF16)
            part_copy[h - NEAR].start()
        for h in range(NEAR, HEADS):
            k_copy[h].start()
            v_copy[h].start()

    u[...] = dot_nt(item_ref[:, own_cols], w_ref[...])
    per_user = width // users
    for j in range(users // 2):
        item_t[j] = item_ref[:, j * 2 * per_user : (j + 1) * 2 * per_user].T

    w_y[0].wait_recv()
    w_far[0].start()

    def look_back(h):
        k_copy[h].wait_recv()
        weight, slope = gates(dot_nt(q_ref[:, head(h)], ok[h]), seen)
        sl_x[h] = slope
        v_copy[h].wait_recv()
        att[:, head(h)] += dot_nn(weight, ov[h])

    @pl.when(ctx == 1)
    def _():
        look_back(0)

    w_y[1].wait_recv()
    w_far[1].start()

    @pl.when(ctx == 1)
    def _():
        for h in range(1, NEAR):
            look_back(h)
        for h in range(NEAR, HEADS):
            part_copy[h - NEAR].wait_recv()
            att[:, head(h)] += part_in[h - NEAR].astype(F32)

    for copy in w_core + w_far:
        copy.wait_recv()
    for part in range(4):
        part_cols = slice(part * w_part, (part + 1) * w_part)
        u[:, part_cols] += dot_nt(item_ref[:, other_cols], wbuf[part])

    attended = att[...]
    centered = attended - jnp.mean(attended, axis=-1, keepdims=True)
    inv_std = lax.rsqrt(jnp.mean(centered * centered, axis=-1, keepdims=True) + norm_eps)
    normed = centered * inv_std
    gate_f = gate_ref[...].astype(F32)
    mixed_out = (normed * gate_f).astype(BF16)
    item_proj = u[...]
    logits = jnp.sum(mixed_out.astype(F32) * item_proj, axis=-1, keepdims=True)

    stat_copy.wait_recv()
    onehot_x = (
        lax.broadcasted_iota(jnp.int32, (REQS, rows), 0) == stat_in[0:1].astype(jnp.int32)
    ).astype(F32)
    inv_sum = jnp.sum(onehot * inv_prop + onehot_x * stat_in[1:2], axis=1, keepdims=True)
    live_count = jnp.sum(onehot * live_f + onehot_x * stat_in[2:3], axis=1, keepdims=True)
    some = live_count > 0
    ratio = jnp.where(some, live_count / jnp.where(some, inv_sum, 1.0), 0.0)
    event_weight = inv_prop * jnp.sum(onehot * ratio, axis=0, keepdims=True)
    eye = row_i == col_i
    weight_col = jnp.sum(jnp.where(eye, event_weight, 0.0), axis=1, keepdims=True)
    label_col = jnp.sum(jnp.where(eye, lab_ref[...].astype(F32), 0.0), axis=1, keepdims=True)
    grad_logits = weight_col * (jax.nn.sigmoid(logits) - label_col)
    weighted = (grad_logits * mixed_out.astype(F32)).astype(BF16)
    for half in range(2):
        mixed[half] = weighted[:, half * cols : (half + 1) * cols]
    halves = [1 - ctx, ctx]
    piece = feats // PIECES
    c_copy = [remote(gw.at[1 - core, o], r_core.at[o], cs.at[o], cr.at[o], c_peer) for o in range(PIECES)]
    y_copy = [remote(s_y.at[o], r_y.at[o], ys.at[o], yr.at[o], y_peer) for o in range(PIECES)]
    z_copy = [
        [
            remote(
                s_z.at[o, lax.rem(zz + i + 1, nz)], r_z.at[o, i], zs.at[o, i], zr.at[o, i], z_peers[i]
            )
            for i in range(nz - 1)
        ]
        for o in range(PIECES)
    ]
    x_copy = [remote(s_x.at[o], r_x.at[o], xs.at[o], xr.at[o], x_peer) for o in range(PIECES // 2)]
    def weight_grad(o):
        for j in range(users // 2):
            chunk = dot_nn(item_t[j], mixed[halves[o]]).astype(BF16)
            for c in range(2):
                for p in range(PIECES // 2):
                    gw[c, o * PIECES // 2 + p, j % 2, j // 2] = chunk[
                        c * per_user : (c + 1) * per_user, p * piece : (p + 1) * piece
                    ]
        for p in range(PIECES // 2):
            c_copy[o * PIECES // 2 + p].start()

    weight_grad(0)
    weight_grad(1)

    def after_core(o):
        c_copy[o].wait_recv()
        s_y[o] = (gw[core, o, 1 - yy].astype(F32) + r_core[o, 1 - yy].astype(F32)).astype(BF16)
        y_copy[o].start()

    def after_y(o):
        y_copy[o].wait_recv()
        mine = gw[core, o, yy].astype(F32) + r_core[o, yy].astype(F32)
        s_z[o] = (mine + r_y[o].astype(F32)).astype(BF16)
        for copy in z_copy[o]:
            copy.start()

    def after_z(o):
        total = gw[core, o, yy, zz].astype(F32) + r_core[o, yy, zz].astype(F32)
        total += r_y[o, zz].astype(F32)
        for i in range(nz - 1):
            z_copy[o][i].wait_recv()
            total += r_z[o, i].astype(F32)
        if o < PIECES // 2:
            s_x[o] = total.astype(BF16)
            x_copy[o].start()
        else:
            fin[o - PIECES // 2] = total

    def backward(h):
        grad_scores = (dot_nt(da[h], v_ref[:, head(h)]) * sl[h]).astype(BF16)
        dq_ref[:, head(h)] = dot_nn(grad_scores, k_ref[:, head(h)]) * factor
        dk_ref[:, head(h)] = dot_tn(grad_scores, q_ref[:, head(h)]) * factor
        dv_ref[:, head(h)] = dot_tn(wt[h], da[h])

    def cross_query(h):
        grad_scores = (dot_nt(da[h], ov[h]) * sl_x[h]).astype(BF16)
        dq_ref[:, head(h)] += dot_nn(grad_scores, ok[h]) * factor

    def cross_key(h):
        da_copy[h].wait_recv()
        grad_scores = (dot_nt(oda[h], v_ref[:, head(h)]) * sl_x[h]).astype(BF16)
        dk_ref[:, head(h)] += dot_tn(grad_scores, oq[h]) * factor
        dv_ref[:, head(h)] += dot_tn(wt_x[h], oda[h])

    for o in range(PIECES):
        after_core(o)

    grad_mixed = grad_logits * item_proj
    dgate_ref[...] = grad_mixed * normed
    grad_normed = grad_mixed * gate_f
    grad_attn = (
        grad_normed
        - jnp.mean(grad_normed, axis=-1, keepdims=True)
        - normed * jnp.mean(grad_normed * normed, axis=-1, keepdims=True)
    ) * inv_std
    for h in range(HEADS):
        da[h] = grad_attn[:, head(h)].astype(BF16)

    @pl.when(ctx == 1)
    def _():
        for h in range(HEADS):
            da_copy[h].start()

    for h in range(HEADS):
        backward(h)
        if h > 0:
            after_y(h - 1)

    @pl.when(ctx == 0)
    def _():
        for h in range(NEAR):
            cross_scores(h)

    @pl.when(ctx == 1)
    def _():
        for h in range(NEAR):
            cross_query(h)

    after_y(3)

    for o in range(PIECES // 2):
        after_z(o)

    @pl.when(ctx == 1)
    def _():
        for h in range(NEAR, HEADS):
            k_copy[h].wait_recv()
            v_copy[h].wait_recv()
            sl_x[h] = gates(dot_nt(q_ref[:, head(h)], ok[h]), seen)[1]
            cross_query(h)

    @pl.when(ctx == 0)
    def _():
        for h in range(HEADS):
            cross_key(h)

    for o in range(PIECES // 2, PIECES):
        after_z(o)

    @pl.when(ctx == 0)
    def _():
        for h in range(HEADS):
            k_copy[h].wait_send()
            v_copy[h].wait_send()
        for copy in part_copy:
            copy.wait_send()

    @pl.when(ctx == 1)
    def _():
        for h in range(HEADS):
            q_copy[h].wait_send()
            da_copy[h].wait_send()

    for o in range(PIECES // 2):
        x_copy[o].wait_recv()
        dw_ref[:, o * piece : (o + 1) * piece] = fin[o] + r_x[o].astype(F32)
    for copy in [stat_copy] + x_copy + w_all + c_copy + y_copy + sum(z_copy, []):
        copy.wait_send()


def write_kernel(a, b, c, d, e, a_out, b_out, c_out, d_out, e_out, sems):
    copies = [
        pltpu.make_async_copy(src, dst, sems.at[i])
        for i, (src, dst) in enumerate(((a, a_out), (b, b_out), (c, c_out), (d, d_out), (e, e_out)))
    ]
    for copy in copies:
        copy.start()
    for copy in copies:
        copy.wait()


def fused(
    users, queries, key_rows, value_rows, gate_rows, item_emb, labels, propensity, requests, lengths, w_out
):
    _, rows, feats = queries.shape
    width = item_emb.shape[2]
    per_user = width // users
    nz = users // 4
    cols = feats // 2
    piece = feats // PIECES
    dma = pltpu.SemaphoreType.DMA
    block = (HEADS, rows, HEAD_DIM)
    square = (HEADS, rows, rows)
    vmem = pl.BlockSpec(memory_space=pltpu.VMEM)
    hbm = pl.BlockSpec(memory_space=pltpu.HBM)
    row = (1, rows)
    out = jax.ShapeDtypeStruct((rows, feats), F32)
    operands = [
        pltpu.with_memory_space_constraint(x, pltpu.HBM)
        for x in (
            queries[0], key_rows[0], value_rows[0], gate_rows[0], item_emb[0],
            labels, propensity, requests, w_out,
        )
    ]
    results = pl.pallas_call(
        functools.partial(fused_kernel, users),
        out_shape=[out, out, out, out, jax.ShapeDtypeStruct((per_user, cols), F32)],
        in_specs=[pl.BlockSpec(memory_space=pltpu.SMEM)] + [hbm] * 9,
        out_specs=[vmem] * 5,
        scratch_shapes=[pltpu.VMEM((rows, feats), BF16)] * 4
        + [
            pltpu.VMEM((rows, width), BF16),
            pltpu.VMEM(row, jnp.int32),
            pltpu.VMEM(row, F32),
            pltpu.VMEM(row, jnp.int32),
            pltpu.VMEM((feats, width // 2), BF16),
            dma((9,)),
            pltpu.VMEM(block, BF16),
            pltpu.VMEM(block, BF16),
            pltpu.VMEM(block, BF16),
            pltpu.VMEM(block, BF16),
            pltpu.VMEM((4, feats // 4, width // 2), BF16),
            pltpu.VMEM((8, rows), F32),
            pltpu.VMEM((8, rows), F32),
            pltpu.VMEM((HEADS - NEAR, rows, HEAD_DIM), BF16),
            pltpu.VMEM((HEADS - NEAR, rows, HEAD_DIM), BF16),
            pltpu.VMEM((2, rows, cols), BF16),
            pltpu.VMEM((users // 2, 2 * per_user, rows), BF16),
            pltpu.VMEM(square, BF16),
            pltpu.VMEM(square, F32),
            pltpu.VMEM(square, BF16),
            pltpu.VMEM(square, F32),
            pltpu.VMEM((rows, feats), F32),
            pltpu.VMEM((rows, feats), F32),
            pltpu.VMEM(block, BF16),
            pltpu.VMEM((2, PIECES, 2, nz, per_user, piece), BF16),
            pltpu.VMEM((PIECES, 2, nz, per_user, piece), BF16),
            pltpu.VMEM((PIECES, nz, per_user, piece), BF16),
            pltpu.VMEM((PIECES, nz, per_user, piece), BF16),
            pltpu.VMEM((PIECES, nz, per_user, piece), BF16),
            pltpu.VMEM((PIECES, nz - 1, per_user, piece), BF16),
            pltpu.VMEM((PIECES // 2, per_user, piece), F32),
            pltpu.VMEM((PIECES // 2, per_user, piece), BF16),
            pltpu.VMEM((PIECES // 2, per_user, piece), BF16),
        ]
        + [dma((HEADS,))] * 8
        + [dma((8,))] * 2
        + [dma] * 2
        + [dma((HEADS - NEAR,))] * 2
        + [dma((PIECES,))] * 4
        + [dma((PIECES, nz - 1))] * 2
        + [dma((PIECES // 2,))] * 2,
        compiler_params=pltpu.CompilerParams(
            collective_id=0, has_side_effects=True, vmem_limit_bytes=48 * 1024 * 1024
        ),
        cost_estimate=pl.CostEstimate(
            flops=4 * 10**9, bytes_accessed=5 * 10**6, transcendentals=10**6
        ),
    )(lengths, *operands)
    dq, dk, dv, dgate, dw = pl.pallas_call(
        write_kernel,
        out_shape=[jax.ShapeDtypeStruct(r.shape, F32) for r in results],
        in_specs=[vmem] * 5,
        out_specs=[hbm] * 5,
        scratch_shapes=[dma((5,))],
        compiler_params=pltpu.CompilerParams(vmem_limit_bytes=4 * 1024 * 1024),
        cost_estimate=pl.CostEstimate(flops=0, bytes_accessed=2 * 10**6, transcendentals=0),
    )(*[pltpu.with_memory_space_constraint(r, pltpu.VMEM) for r in results])
    return dq[None], dk[None], dv[None], dgate[None], dw.T


def solution(mesh):
    in_specs = (
        P("user", "ctx", None),
        P("user", "ctx", None),
        P("user", "ctx", None),
        P("user", "ctx", None),
        P("user", "ctx", None),
        P("user", "ctx"),
        P("user", "ctx"),
        P("user", "ctx"),
        P("user"),
        P(None, "ctx"),
    )
    out_specs = (
        P("user", "ctx", None),
        P("user", "ctx", None),
        P("user", "ctx", None),
        P("user", "ctx", None),
        P("ctx", "user"),
    )
    users = mesh.shape["user"]
    two_blocks = mesh.shape["ctx"] == 2 and users % 8 == 0
    step = functools.partial(fused, users) if two_blocks else local
    return jax.shard_map(step, mesh=mesh, in_specs=in_specs, out_specs=out_specs, check_vma=False)
```
